256 devices in a mesh: hid: 4 (over z_lo), ffn: 64 (over x, z_hi, y, core).
Axes of the slice: x: 4, y: 4, z: 8 (z_hi: 2, z_lo: 4; z = z_hi * 4 + z_lo), core: 2. Of those that a mesh axis runs over, the one named last changes fastest.
Arguments:
- inputs: bfloat16 [512, 8192], P('ffn', 'hid'), may hold values from -3 to 3
- gate_grad: bfloat16 [512, 53248], P('hid', 'ffn'), may hold values from -1.1953125 to 1.1953125
- up_grad: bfloat16 [512, 53248], P('hid', 'ffn'), may hold values from -1.1953125 to 1.1953125
- gate_codes: bfloat16 [8192, 53248], P('hid', 'ffn'), may hold values from -127 to 127, as said below
- up_codes: bfloat16 [8192, 53248], P('hid', 'ffn'), may hold values from -127 to 127, as said below
- gate_scale: float32 [53248], P('ffn'), as said below
- up_scale: float32 [53248], P('ffn'), as said below
- gate_down: float32 [8192, 16], P('hid'), may hold values from -0.0625 to 0.0625
- gate_lift: float32 [16, 53248], P(None, 'ffn'), may hold values from -0.06 to 0.06
- up_down: float32 [8192, 16], P('hid'), may hold values from -0.0625 to 0.0625
- up_lift: float32 [16, 53248], P(None, 'ffn'), may hold values from -0.06 to 0.06
Outputs:
- input_gradient_rows: bfloat16 [512, 8192], P('ffn', 'hid')
- gate_reducer_gradient: float32 [8192, 16], P('hid')
- gate_expander_gradient: float32 [16, 53248], P(None, 'ffn')
- upward_reducer_gradient: float32 [8192, 16], P('hid')
- upward_expander_gradient: float32 [16, 53248], P(None, 'ffn')
The draws below stay inside these ranges and needn't reach their ends.
Inputs may be any that keep to these rules, and one draw needn't show every extreme that they name: `gate_codes`: whole numbers. `up_codes`: whole numbers. `gate_scale`: between 0.5 and 2 times 1 / (73 sqrt(8192)). `up_scale`: between 0.5 and 2 times 1 / (73 sqrt(8192)).
All inputs are finite; a program needn't handle non-finite values.
Results may differ from the reference program's by a relative error of at most 0.014.
Values may be sent and summed in bfloat16 or wider, within the bound.
No kernel may reach another device: no remote copies, remote signals or barrier semaphores. Data moves between devices by JAX's collectives and lax.ppermute only.
A program may use at most 64 MiB of HBM per device.

```python
import math
import jax
import jax.numpy as jnp
from jax import lax

D = 8192
FF = 53248
RANK = 16
TOKENS = 512


def draw_gate_codes(key, part):
    key = jax.random.fold_in(key, 11)
    return jax.random.randint(key, (D, FF), -127, 128).astype(jnp.float32).astype(jnp.bfloat16)


def draw_up_codes(key, part):
    key = jax.random.fold_in(key, 12)
    return jax.random.randint(key, (D, FF), -127, 128).astype(jnp.float32).astype(jnp.bfloat16)


def column_scales(key):
    spread = jax.random.uniform(key, (FF,), jnp.float32, math.log(0.5), math.log(2.0))
    return jnp.exp(spread) / (73.0 * math.sqrt(D))


def draw_gate_scale(key, part):
    key = jax.random.fold_in(key, 13)
    return column_scales(key)


def draw_up_scale(key, part):
    key = jax.random.fold_in(key, 14)
    return column_scales(key)


def steps_of(key, dims, shards, low, top_value):
    factor_of, own = 1.0, jax.random.fold_in(key, 6)
    for position, blocks in shards:
        heights = jnp.exp(jax.random.uniform(jax.random.fold_in(own, position), (blocks,), jnp.float32, low / len(shards), top_value / len(shards)))
        factor_of = factor_of * jnp.repeat(heights, dims[position] // blocks).reshape([-1 if axis == position else 1 for axis in range(len(dims))])
    return factor_of


def normal_values(rng, shape, width, most, split=(), held_as=jnp.bfloat16):
    array = width * jax.random.normal(rng, shape, jnp.float32)
    if split:
        array = array * steps_of(rng, shape, split, -0.22, 0.18)
    return jnp.clip(array, -most, most).astype(held_as)


def setup_inputs(seed: int = 0) -> dict:
    splits = jax.random.split(jax.random.key(seed), 12)
    inputs = normal_values(splits[0], (TOKENS, D), 0.5, 3.0, ((0, 64), (1, 4)))
    gate_grad = normal_values(splits[1], (TOKENS, FF), 0.2, 1.1953125, ((0, 4), (1, 64)))
    up_grad = normal_values(splits[2], (TOKENS, FF), 0.2, 1.1953125, ((0, 4), (1, 64)))
    gate_codes = draw_gate_codes(jax.random.fold_in(splits[11], 71), 0)
    up_codes = draw_up_codes(jax.random.fold_in(splits[11], 71), 0)
    gate_scale = draw_gate_scale(jax.random.fold_in(splits[11], 71), 0)
    up_scale = draw_up_scale(jax.random.fold_in(splits[11], 71), 0)
    gate_down = normal_values(splits[7], (D, RANK), D ** -0.5, 0.0625, ((0, 4),), jnp.float32)
    gate_lift = normal_values(splits[8], (RANK, FF), 0.01, 0.06, ((1, 64),), jnp.float32)
    up_down = normal_values(splits[9], (D, RANK), D ** -0.5, 0.0625, ((0, 4),), jnp.float32)
    up_lift = normal_values(splits[10], (RANK, FF), 0.01, 0.06, ((1, 64),), jnp.float32)
    return {"inputs": inputs, "gate_grad": gate_grad, "up_grad": up_grad, "gate_codes": gate_codes, "up_codes": up_codes, "gate_scale": gate_scale, "up_scale": up_scale, "gate_down": gate_down, "gate_lift": gate_lift, "up_down": up_down, "up_lift": up_lift}


ADAPTER_SCALE = 2.0


def precise_product(left, right):
    return jnp.dot(left, right, precision=lax.Precision.HIGHEST, preferred_element_type=jnp.float32)


def reference(inputs, gate_grad, up_grad, gate_codes, up_codes, gate_scale, up_scale, gate_down, gate_lift, up_down, up_lift):
    gate_weight = (gate_codes.astype(jnp.float32) * gate_scale).astype(jnp.bfloat16)
    up_weight = (up_codes.astype(jnp.float32) * up_scale).astype(jnp.bfloat16)
    gate_dequantized = gate_grad.astype(jnp.float32)
    upward_dequantized = up_grad.astype(jnp.float32)
    gate_backward_signal = precise_product(gate_dequantized, gate_lift.T)
    upward_backward_signal = precise_product(upward_dequantized, up_lift.T)
    frozen_contribution = jnp.dot(gate_grad, gate_weight.T, preferred_element_type=jnp.float32)
    frozen_contribution = frozen_contribution + jnp.dot(up_grad, up_weight.T, preferred_element_type=jnp.float32)
    adapter_contribution = precise_product(gate_backward_signal, gate_down.T) + precise_product(upward_backward_signal, up_down.T)
    input_gradient_rows = (frozen_contribution + ADAPTER_SCALE * adapter_contribution).astype(jnp.bfloat16)
    input_widened = inputs.astype(jnp.float32)
    gate_narrow_activation = precise_product(input_widened, gate_down)
    upward_narrow_activation = precise_product(input_widened, up_down)
    gate_expander_gradient = ADAPTER_SCALE * precise_product(gate_narrow_activation.T, gate_dequantized)
    upward_expander_gradient = ADAPTER_SCALE * precise_product(upward_narrow_activation.T, upward_dequantized)
    gate_reducer_gradient = ADAPTER_SCALE * precise_product(input_widened.T, gate_backward_signal)
    upward_reducer_gradient = ADAPTER_SCALE * precise_product(input_widened.T, upward_backward_signal)
    return (input_gradient_rows, gate_reducer_gradient, gate_expander_gradient, upward_reducer_gradient, upward_expander_gradient)
```

```python
import jax
import jax.numpy as jnp
from jax import lax
from jax.sharding import Mesh, PartitionSpec as P

ADAPTER_SCALE = 2.0
FFN = ("x", "zh", "y", "core")
F32, BF16 = jnp.float32, jnp.bfloat16


def swap(value, axis, mask):
    size = lax.axis_size(axis)
    return lax.ppermute(value, axis, [(i, i ^ mask) for i in range(size)])


def xor_order(value, dim, index):
    size, step = value.shape[dim], 1
    while step < size:
        order = [j ^ step for j in range(size)]
        moved = jnp.concatenate([lax.slice_in_dim(value, j, j + 1, axis=dim) for j in order], dim)
        value = jnp.where((index & step) != 0, moved, value)
        step *= 2
    return value


def pair_first(value, dim, index):
    other = lax.dynamic_index_in_dim(value, 1 - index, dim, keepdims=False)
    own = lax.dynamic_index_in_dim(value, index, dim, keepdims=False)
    return other, own


def dot(left, right, contract):
    return lax.dot_general(left, right, (contract, ((), ())), preferred_element_type=F32)


def sum_over(value, axis):
    size = lax.axis_size(axis)
    parts = [value] + [swap(value, axis, k) for k in range(1, size)]
    total = parts[0]
    for part in parts[1:]:
        total = total + part
    return total


def gather_over(value, axis):
    size = lax.axis_size(axis)
    return jnp.stack([value] + [swap(value, axis, k) for k in range(1, size)])


def per_device(
    inputs, gate_grad, up_grad, gate_codes, up_codes, gate_scale, up_scale,
    gate_down, gate_lift, up_down, up_lift,
):
    hid = lax.axis_index("hid")
    x, zh, y, core = (lax.axis_index(name) for name in FFN)

    scaled = jnp.stack(
        [
            (gate_grad.astype(F32) * gate_scale).astype(BF16),
            (up_grad.astype(F32) * up_scale).astype(BF16),
        ]
    ).reshape(2, 2, 4, 2, 8, 832)
    phases = []
    for half in pair_first(scaled, 1, zh):
        other, own = pair_first(half, 2, core)
        phases.append(jnp.stack([other, own], 1).reshape(2, 64, 832))

    tokens = gather_over(inputs, "zh").reshape(16, 2048)
    tokens = gather_over(tokens, "x").reshape(64, 2048)
    tokens = gather_over(tokens, "y").reshape(256, 2048)

    back = jnp.concatenate(
        [
            dot(gate_grad, gate_lift.astype(BF16), ((1,), (1,))),
            dot(up_grad, up_lift.astype(BF16), ((1,), (1,))),
        ],
        1,
    ).reshape(8, 2, 8, 32)
    other, own = pair_first(back, 1, core)
    back = (own + swap(other, "core", 1)).reshape(64, 32)
    back = sum_over(back, "x")
    back = sum_over(back, "y")
    back = sum_over(back, "zh")
    back = gather_over(back, "hid").reshape(4, 2, 4, 8, 32)
    back = xor_order(xor_order(xor_order(back, 0, hid ^ x), 1, zh), 2, y)
    back = back.transpose(2, 0, 1, 3, 4).reshape(256, 32)
    down = jnp.concatenate([gate_down, up_down], 1).astype(BF16)
    adapter = ADAPTER_SCALE * dot(back[:8].astype(BF16), down, ((1,), (1,)))
    reducer = ADAPTER_SCALE * dot(tokens, back.astype(BF16), ((0,), (0,)))
    reducer = reducer + swap(reducer, "core", 1)

    low = sum_over(dot(tokens, down, ((1,), (0,))).astype(BF16), "hid").astype(BF16)
    low = low.reshape(4, 4, 2, 8, 32)
    low = xor_order(xor_order(low, 0, y), 1, x)
    low = jnp.stack([swap(low, "core", 1), low])
    low = low.transpose(3, 2, 0, 1, 4, 5)[::-1].reshape(2, 256, 32)

    kept = []
    expander = None
    for phase, mine in enumerate(phases):
        grads = lax.all_gather(mine, "hid", axis=1, tiled=True)
        part = dot(grads[0], gate_codes, ((1,), (1,))) + dot(grads[1], up_codes, ((1,), (1,)))
        part = part.astype(BF16).reshape(4, 2, 32, 2048)
        summed = part[:, 1].astype(F32) + swap(part[:, 0], "core", 1).astype(F32)
        summed = summed.astype(BF16).reshape(128, 2048)
        landed = lax.all_to_all(summed, ("x", "y"), split_axis=0, concat_axis=0, tiled=True)
        kept.append(landed.astype(F32).reshape(16, 8, 2048).sum(0))
        term = [
            dot(low[phase, :, 16 * k : 16 * k + 16], grads[k], ((0,), (0,))) for k in range(2)
        ]
        expander = term if expander is None else [a + b for a, b in zip(expander, term)]
    arrived = swap(kept[0].astype(BF16), "zh", 1)
    rows = (kept[1] + arrived.astype(F32) + adapter).astype(BF16)
    return (
        rows,
        reducer[:, :16],
        ADAPTER_SCALE * expander[0] / gate_scale,
        reducer[:, 16:],
        ADAPTER_SCALE * expander[1] / up_scale,
    )


def solution(mesh):
    whole = Mesh(mesh.devices.reshape(4, 4, 2, 4, 2), ("hid",) + FFN)
    placed = (
        P(FFN, "hid"), P("hid", FFN), P("hid", FFN), P("hid", FFN), P("hid", FFN),
        P(FFN), P(FFN), P("hid", None), P(None, FFN), P("hid", None), P(None, FFN),
    )
    return jax.shard_map(
        per_device,
        mesh=whole,
        in_specs=placed,
        out_specs=(P(FFN, "hid"), P("hid", None), P(None, FFN), P("hid", None), P(None, FFN)),
        check_vma=False,
    )
```

```python
import jax
import jax.numpy as jnp
from jax import lax
from jax.experimental import pallas as pl
from jax.experimental.pallas import tpu as pltpu
from jax.sharding import Mesh, PartitionSpec as P

ADAPTER_SCALE = 2.0
FFN = ("x", "zh", "y", "core")
F32, BF16 = jnp.float32, jnp.bfloat16
UNITS, FEATS, STEP = 832, 2048, 256
BY_ROWS = (((1,), (1,)), ((), ()))
BY_COLUMNS = (((0,), (0,)), ((), ()))
SMEM = pl.BlockSpec(memory_space=pltpu.SMEM)
VMEM = pl.BlockSpec(memory_space=pltpu.VMEM)


def swap(value, axis, mask):
    size = lax.axis_size(axis)
    return lax.ppermute(value, axis, [(i, i ^ mask) for i in range(size)])


def gather_over(value, axis):
    return [value] + [swap(value, axis, k) for k in range(1, lax.axis_size(axis))]


def xor_order(value, dim, index):
    size, step = value.shape[dim], 1
    while step < size:
        order = [j ^ step for j in range(size)]
        moved = jnp.concatenate([lax.slice_in_dim(value, j, j + 1, axis=dim) for j in order], dim)
        value = jnp.where((index & step) != 0, moved, value)
        step *= 2
    return value


def dot(left, right, how):
    return lax.dot_general(left, right, how, preferred_element_type=F32)


def prep_kernel(place, gate, up, gate_scale, up_scale, gate_lift, up_lift, far, near, back_other, back_own):
    zh, core = place[0], place[1]
    for k, (grad, scale) in enumerate(((gate, gate_scale), (up, up_scale))):
        rows = (grad[...].astype(F32) * scale[...]).reshape(2, 4, 2, 8, UNITS)
        first, second = rows[0], rows[1]
        for out, half in (
            (far, jnp.where(zh == 0, second, first)),
            (near, jnp.where(zh == 0, first, second)),
        ):
            other = jnp.where(core == 0, half[:, 1], half[:, 0]).reshape(32, UNITS)
            own = jnp.where(core == 0, half[:, 0], half[:, 1]).reshape(32, UNITS)
            out[k, 0] = other.astype(BF16)
            out[k, 1] = own.astype(BF16)
    none = jnp.zeros((16, UNITS), F32)
    back = dot(gate[...], jnp.concatenate([gate_lift[...], none], 0).astype(BF16), BY_ROWS)
    back += dot(up[...], jnp.concatenate([none, up_lift[...]], 0).astype(BF16), BY_ROWS)
    back = back.reshape(8, 2, 8, 32)
    back_other[...] = jnp.where(core == 0, back[:, 1], back[:, 0]).reshape(64, 32)
    back_own[...] = jnp.where(core == 0, back[:, 0], back[:, 1]).reshape(64, 32)


def prep(place, *arrays):
    half = jax.ShapeDtypeStruct((2, 2, 32, UNITS), BF16)
    back = jax.ShapeDtypeStruct((64, 32), F32)
    return pl.pallas_call(
        prep_kernel,
        out_shape=(half, half, back, back),
        in_specs=[SMEM] + [VMEM] * 6,
        out_specs=(VMEM,) * 4,
        cost_estimate=pl.CostEstimate(flops=14_000_000, bytes_accessed=1_200_000, transcendentals=0),
        name="prep",
    )(place, *arrays)


def product_kernel(place, r0, r1, r2, r3a, r3b, gate_codes, up_codes, out, grads):
    @pl.when(pl.program_id(0) == 0)
    def _():
        for k in range(2):
            for c in range(2):
                for j, block in enumerate((r0, r1, r2)):
                    grads[k, c, place[0] ^ j] = block[k, c]
                grads[k, c, place[0] ^ 3] = r3a[k, c] + r3b[k, c]

    total = dot(grads[0].reshape(256, UNITS), gate_codes[...], BY_ROWS)
    total += dot(grads[1].reshape(256, UNITS), up_codes[...], BY_ROWS)
    out[...] = total.astype(BF16).reshape(2, 128, STEP)


def product(place, blocks, gate_codes, up_codes):
    whole = pl.BlockSpec((2, 2, 32, UNITS), lambda i: (0, 0, 0, 0))
    codes = pl.BlockSpec((STEP, UNITS), lambda i: (i, 0))
    return pl.pallas_call(
        product_kernel,
        grid=(FEATS // STEP,),
        out_shape=(
            jax.ShapeDtypeStruct((2, 128, FEATS), BF16),
            jax.ShapeDtypeStruct((2, 2, 4, 32, UNITS), BF16),
        ),
        in_specs=[SMEM] + [whole] * 5 + [codes] * 2,
        out_specs=(
            pl.BlockSpec((2, 128, STEP), lambda i: (0, 0, i)),
            pl.BlockSpec((2, 2, 4, 32, UNITS), lambda i: (0, 0, 0, 0, 0)),
        ),
        compiler_params=pltpu.CompilerParams(vmem_limit_bytes=32 << 20),
        cost_estimate=pl.CostEstimate(flops=1_750_000_000, bytes_accessed=9_700_000, transcendentals=0),
        name="product",
    )(place, *blocks, gate_codes, up_codes)


def expander_kernel(low, far, near, gate_scale, up_scale, gate_out, up_out):
    for k, (out, scale) in enumerate(((gate_out, gate_scale), (up_out, up_scale))):
        total = dot(low[0], far[k].reshape(256, UNITS), BY_COLUMNS)
        total += dot(low[1], near[k].reshape(256, UNITS), BY_COLUMNS)
        out[...] = ADAPTER_SCALE * total[16 * k : 16 * k + 16] / scale[...]


def expander(*arrays):
    out = jax.ShapeDtypeStruct((16, UNITS), F32)
    return pl.pallas_call(
        expander_kernel,
        out_shape=(out, out),
        in_specs=[VMEM] * 5,
        out_specs=(VMEM, VMEM),
        compiler_params=pltpu.CompilerParams(vmem_limit_bytes=32 << 20),
        cost_estimate=pl.CostEstimate(flops=55_000_000, bytes_accessed=2_000_000, transcendentals=0),
        name="expander",
    )(*arrays)


def gather_hid(value):
    two = swap(value, "hid", 2)
    one = swap(value, "hid", 1)
    middle = lax.ppermute(value, "hid", [(1, 2), (2, 1)])
    ends = lax.ppermute(two, "hid", [(1, 0), (2, 3)])
    return value, one, two, middle, ends


def per_device(
    inputs, gate_grad, up_grad, gate_codes, up_codes, gate_scale, up_scale,
    gate_down, gate_lift, up_down, up_lift,
):
    hid = lax.axis_index("hid")
    x, zh, y, core = (lax.axis_index(name) for name in FFN)
    gate_scale, up_scale = gate_scale.reshape(1, UNITS), up_scale.reshape(1, UNITS)

    far, near, back_other, back_own = prep(
        jnp.stack([zh, core]), gate_grad, up_grad, gate_scale, up_scale, gate_lift, up_lift
    )
    far_blocks = gather_hid(far)
    near_blocks = gather_hid(near)

    tokens = jnp.concatenate(gather_over(inputs, "zh"), 0)
    back = (back_own + swap(back_other, "core", 1)).reshape(16, 128)
    parts = gather_over(jnp.concatenate([tokens, back.astype(BF16)], 1), "x")
    tokens = jnp.concatenate([part[:, :FEATS] for part in parts], 0)
    back = sum(part[:, FEATS:].astype(F32) for part in parts)
    back = jnp.pad(back.astype(BF16), ((0, 48), (0, 0)))
    parts = gather_over(jnp.concatenate([tokens, back], 1), "y")
    tokens = jnp.concatenate([part[:, :FEATS] for part in parts], 0)
    back = sum(part[:16, FEATS:].astype(F32) for part in parts)
    back = (back + swap(back, "zh", 1)).reshape(64, 32)

    down = jnp.concatenate([gate_down, up_down], 1).astype(BF16)
    low = dot(tokens, down, (((1,), (0,)), ((), ())))
    parts = gather_over(jnp.concatenate([low, back], 0).astype(BF16), "hid")
    low = sum(part[:256].astype(F32) for part in parts).astype(BF16)
    back = jnp.stack([part[256:] for part in parts]).reshape(4, 2, 4, 8, 32)
    back = xor_order(xor_order(xor_order(back, 0, hid ^ x), 1, zh), 2, y)
    back = back.transpose(2, 0, 1, 3, 4).reshape(256, 32)

    adapter = ADAPTER_SCALE * dot(back[:8], down, BY_ROWS)
    reducer = ADAPTER_SCALE * dot(tokens, back, BY_COLUMNS)
    reducer = reducer + swap(reducer, "core", 1)

    low = low.reshape(4, 4, 2, 8, 32)
    low = xor_order(xor_order(low, 0, y), 1, x)
    low = jnp.stack([swap(low, "core", 1), low])
    low = low.transpose(3, 0, 2, 1, 4, 5)[::-1].reshape(2, 256, 32)

    kept, grads = [], []
    for blocks in (far_blocks, near_blocks):
        part, assembled = product(hid.reshape(1), blocks, gate_codes, up_codes)
        grads.append(assembled)
        summed = part[1].astype(F32) + swap(part[0], "core", 1).astype(F32)
        landed = lax.all_to_all(
            summed.astype(BF16), ("x", "y"), split_axis=0, concat_axis=0, tiled=True
        )
        kept.append(landed.astype(F32).reshape(16, 8, FEATS).sum(0))
    gate_expander, up_expander = expander(low, *grads, gate_scale, up_scale)
    arrived = swap(kept[0].astype(BF16), "zh", 1)
    rows = (kept[1] + arrived.astype(F32) + adapter).astype(BF16)
    return rows, reducer[:, :16], gate_expander, reducer[:, 16:], up_expander


def solution(mesh):
    whole = Mesh(mesh.devices.reshape(4, 4, 2, 4, 2), ("hid",) + FFN)
    placed = (
        P(FFN, "hid"), P("hid", FFN), P("hid", FFN), P("hid", FFN), P("hid", FFN),
        P(FFN), P(FFN), P("hid", None), P(None, FFN), P("hid", None), P(None, FFN),
    )
    return jax.shard_map(
        per_device,
        mesh=whole,
        in_specs=placed,
        out_specs=(P(FFN, "hid"), P("hid", None), P(None, FFN), P("hid", None), P(None, FFN)),
        check_vma=False,
    )
```

```python
import jax
import jax.numpy as jnp
from jax import lax
from jax.experimental import pallas as pl
from jax.experimental.pallas import tpu as pltpu
from jax.sharding import Mesh, PartitionSpec as P

ADAPTER_SCALE = 2.0
FFN = ("x", "zh", "y", "core")
F32, BF16 = jnp.float32, jnp.bfloat16
UNITS, FEATS, STEP = 832, 2048, 256
PLAIN = (((1,), (0,)), ((), ()))
BY_ROWS = (((1,), (1,)), ((), ()))
BY_COLUMNS = (((0,), (0,)), ((), ()))
SMEM = pl.BlockSpec(memory_space=pltpu.SMEM)
VMEM = pl.BlockSpec(memory_space=pltpu.VMEM)


def swap(value, axis, mask):
    size = lax.axis_size(axis)
    return lax.ppermute(value, axis, [(i, i ^ mask) for i in range(size)])


def gather_over(value, axis):
    return [value] + [swap(value, axis, k) for k in range(1, lax.axis_size(axis))]


def after(values, others):
    return lax.optimization_barrier((values, others))[0]


def dot(left, right, how):
    return lax.dot_general(left, right, how, preferred_element_type=F32)


def one_hot(rows, columns, source):
    row = lax.broadcasted_iota(jnp.int32, (rows, columns), 0)
    column = lax.broadcasted_iota(jnp.int32, (rows, columns), 1)
    return (column == source(row)).astype(F32).astype(BF16)


def prep_kernel(place, gate, up, gate_scale, up_scale, gate_lift, up_lift, far, near, back_other, back_own):
    zh, core = place[0], place[1]

    def source(row):
        half, side = 1 - row // 64, 1 - row // 32 % 2
        return (half ^ zh) * 64 + row // 8 % 4 * 16 + (side ^ core) * 8 + row % 8

    order = one_hot(128, 128, source)
    none = jnp.zeros((16, UNITS), F32)
    lifts = (
        jnp.concatenate([gate_lift[...], none], 0).astype(BF16),
        jnp.concatenate([none, up_lift[...]], 0).astype(BF16),
    )
    back = jnp.zeros((128, 32), F32)
    for k, (grad, scale) in enumerate(((gate, gate_scale), (up, up_scale))):
        rows = dot(order, grad[...], BY_ROWS)
        back += dot(rows.astype(BF16), lifts[k], BY_ROWS)
        rows = (rows * scale[...].reshape(1, UNITS)).astype(BF16).reshape(2, 2, 32, UNITS)
        far[k] = rows[0]
        near[k] = rows[1]
    back = back.reshape(2, 2, 32, 32)
    back_other[...] = back[:, 0].reshape(64, 32)
    back_own[...] = back[:, 1].reshape(64, 32)


def prep(place, *arrays):
    half = jax.ShapeDtypeStruct((2, 2, 32, UNITS), BF16)
    back = jax.ShapeDtypeStruct((64, 32), F32)
    return pl.pallas_call(
        prep_kernel,
        out_shape=(half, half, back, back),
        in_specs=[SMEM] + [VMEM] * 6,
        out_specs=(VMEM,) * 4,
        cost_estimate=pl.CostEstimate(flops=14_000_000, bytes_accessed=1_200_000, transcendentals=0),
        name="prep",
    )(place, *arrays)


def product_kernel(place, r0, r1, r2, r3a, r3b, gate_codes, up_codes, other, own, grads):
    @pl.when(pl.program_id(0) == 0)
    def _():
        for k in range(2):
            for c in range(2):
                for j, block in enumerate((r0, r1, r2)):
                    grads[k, c, place[0] ^ j] = block[k, c]
                grads[k, c, place[0] ^ 3] = r3a[k, c] + r3b[k, c]

    total = dot(grads[0].reshape(256, UNITS), gate_codes[...], PLAIN)
    total += dot(grads[1].reshape(256, UNITS), up_codes[...], PLAIN)
    other[...] = total[:128].astype(BF16)
    own[...] = total[128:].astype(BF16)


def product(place, blocks, gate_codes, up_codes):
    whole = pl.BlockSpec((2, 2, 32, UNITS), lambda i: (0, 0, 0, 0))
    codes = pl.BlockSpec((UNITS, STEP), lambda i: (0, i))
    part = pl.BlockSpec((128, STEP), lambda i: (0, i))
    return pl.pallas_call(
        product_kernel,
        grid=(FEATS // STEP,),
        out_shape=(
            jax.ShapeDtypeStruct((128, FEATS), BF16),
            jax.ShapeDtypeStruct((128, FEATS), BF16),
            jax.ShapeDtypeStruct((2, 2, 4, 32, UNITS), BF16),
        ),
        in_specs=[SMEM] + [whole] * 5 + [codes] * 2,
        out_specs=(part, part, pl.BlockSpec((2, 2, 4, 32, UNITS), lambda i: (0, 0, 0, 0, 0))),
        compiler_params=pltpu.CompilerParams(vmem_limit_bytes=32 << 20),
        cost_estimate=pl.CostEstimate(flops=1_750_000_000, bytes_accessed=9_700_000, transcendentals=0),
        name="product",
    )(place, *blocks, gate_codes, up_codes)


def joined_kernel(place, p0, p1, p2, p3, tokens, down, low_out, adapter, reducer):
    hid_x, y = place[2] ^ place[3], place[4]
    parts = [part[...] for part in (p0, p1, p2, p3)]
    low = sum(part[:256].astype(F32) for part in parts)
    low_out[...] = low.astype(BF16)
    back = jnp.concatenate([part[256:] for part in parts], 0)

    def source(row):
        rel_y, rel_x, half = row // 64, row // 16 % 4, row // 8 % 2
        return ((rel_x ^ hid_x) * 2 + 1 - half) * 32 + (rel_y ^ y) * 8 + row % 8

    back = (ADAPTER_SCALE * dot(one_hot(256, 256, source), back, PLAIN)).astype(BF16)
    adapter[...] = dot(back[:16], down[...], PLAIN)[:8]
    reducer[...] = dot(back, tokens[...], BY_COLUMNS)


def joined(place, parts, tokens, down):
    return pl.pallas_call(
        joined_kernel,
        out_shape=(
            jax.ShapeDtypeStruct((256, 32), BF16),
            jax.ShapeDtypeStruct((8, FEATS), F32),
            jax.ShapeDtypeStruct((32, FEATS), F32),
        ),
        in_specs=[SMEM] + [VMEM] * 6,
        out_specs=(VMEM,) * 3,
        compiler_params=pltpu.CompilerParams(vmem_limit_bytes=32 << 20),
        cost_estimate=pl.CostEstimate(flops=40_000_000, bytes_accessed=1_700_000, transcendentals=0),
        name="joined",
    )(place, *parts, tokens, down)


def expander_kernel(place, low_other, low_own, far, near, gate_scale, up_scale, gate_out, up_out):
    x, y = place[3], place[4]
    lows = []
    for half in (1, 0):
        order = one_hot(
            128,
            256,
            lambda row: (((row // 8 % 4) ^ y) * 4 + ((row // 32) ^ x)) * 16 + half * 8 + row % 8,
        )
        lows.append([dot(order, low[...], PLAIN).astype(BF16) for low in (low_other, low_own)])
    for k, (out, scale) in enumerate(((gate_out, gate_scale), (up_out, up_scale))):
        total = jnp.zeros((32, UNITS), F32)
        for half, grads in enumerate((far, near)):
            for c in range(2):
                total += dot(lows[half][c], grads[k, c].reshape(128, UNITS), BY_COLUMNS)
        out[...] = ADAPTER_SCALE * total[16 * k : 16 * k + 16] / scale[...].reshape(1, UNITS)


def expander(*arrays):
    out = jax.ShapeDtypeStruct((16, UNITS), F32)
    return pl.pallas_call(
        expander_kernel,
        out_shape=(out, out),
        in_specs=[SMEM] + [VMEM] * 6,
        out_specs=(VMEM, VMEM),
        compiler_params=pltpu.CompilerParams(vmem_limit_bytes=32 << 20),
        cost_estimate=pl.CostEstimate(flops=55_000_000, bytes_accessed=2_000_000, transcendentals=0),
        name="expander",
    )(*arrays)


def direct(value):
    middle = lax.ppermute(value, "hid", [(1, 2), (2, 1)])
    return swap(value, "hid", 2), swap(value, "hid", 1), middle


def relay(two):
    return lax.ppermute(two, "hid", [(1, 0), (2, 3)])


def per_device(
    inputs, gate_grad, up_grad, gate_codes, up_codes, gate_scale, up_scale,
    gate_down, gate_lift, up_down, up_lift,
):
    hid = lax.axis_index("hid")
    x, zh, y, core = (lax.axis_index(name) for name in FFN)
    place = jnp.stack([zh, core, hid, x, y])
    down = jnp.concatenate([gate_down.T, up_down.T], 0).astype(BF16)
    down_columns = jnp.concatenate([gate_down, up_down], 1).astype(BF16)

    far, near, back_other, back_own = prep(
        place, gate_grad.T, up_grad.T, gate_scale, up_scale, gate_lift, up_lift
    )
    far_two, far_one, far_middle = direct(far)
    back = (back_own + swap(back_other, "core", 1)).reshape(2, 4, 256)
    payload = jnp.concatenate([inputs, back.reshape(8, 256).astype(BF16)], 1)
    arrived = swap(payload, "zh", 1)
    back = back + arrived[:, FEATS:].astype(F32).reshape(2, 4, 256)[::-1]
    tokens = jnp.concatenate([inputs, arrived[:, :FEATS]], 0)

    payload = jnp.concatenate(
        [tokens, jnp.pad(back.reshape(8, 256).astype(BF16), ((0, 8), (0, 0)))], 1
    )
    payload, near_sent, far_relayed = after(
        (payload, near, far_two), (far_one, far_middle)
    )
    far_ends = relay(far_relayed)
    near_two, near_one, near_middle = direct(near_sent)
    parts = gather_over(payload, "x")
    tokens = jnp.concatenate([part[:, :FEATS] for part in parts], 0)
    back = sum(part[:8, FEATS:].astype(F32) for part in parts)

    payload = jnp.concatenate([tokens, jnp.pad(back.astype(BF16), ((0, 56), (0, 0)))], 1)
    payload, near_relayed = after((payload, near_two), (near_one, near_middle, far_ends))
    near_ends = relay(near_relayed)
    parts = gather_over(payload, "y")
    tokens = jnp.concatenate([part[:, :FEATS] for part in parts], 0)
    back = sum(part[:8, FEATS:].astype(F32) for part in parts).reshape(64, 32)

    low = dot(tokens, down_columns, PLAIN)
    parts = gather_over(jnp.concatenate([low, back], 0).astype(BF16), "hid")
    low, adapter, reducer = joined(place, parts, tokens, down)
    reducer = reducer + swap(reducer, "core", 1)
    low_other = swap(low, "core", 1)

    kept, grads = [], []
    for blocks in (
        (far, far_one, far_two, far_middle, far_ends),
        (near, near_one, near_two, near_middle, near_ends),
    ):
        other, own, assembled = product(hid.reshape(1), blocks, gate_codes.T, up_codes.T)
        grads.append(assembled)
        summed = own.astype(F32) + swap(other, "core", 1).astype(F32)
        landed = lax.all_to_all(
            summed.astype(BF16), ("x", "y"), split_axis=0, concat_axis=0, tiled=True
        )
        kept.append(landed.astype(F32).reshape(16, 8, FEATS).sum(0))
    gate_expander, up_expander = expander(place, low_other, low, *grads, gate_scale, up_scale)
    arrived = swap(kept[0].astype(BF16), "zh", 1)
    rows = (kept[1] + arrived.astype(F32) + adapter).astype(BF16)
    return rows, reducer[:16].T, gate_expander, reducer[16:].T, up_expander


def solution(mesh):
    whole = Mesh(mesh.devices.reshape(4, 4, 2, 4, 2), ("hid",) + FFN)
    placed = (
        P(FFN, "hid"), P("hid", FFN), P("hid", FFN), P("hid", FFN), P("hid", FFN),
        P(FFN), P(FFN), P("hid", None), P(None, FFN), P("hid", None), P(None, FFN),
    )
    return jax.shard_map(
        per_device,
        mesh=whole,
        in_specs=placed,
        out_specs=(P(FFN, "hid"), P("hid", None), P(None, FFN), P("hid", None), P(None, FFN)),
        check_vma=False,
    )
```

```python
import functools

import jax
import jax.numpy as jnp
from jax import lax
from jax.experimental import pallas as pl
from jax.experimental.pallas import tpu as pltpu
from jax.sharding import Mesh, PartitionSpec as P

ADAPTER_SCALE = 2.0
FFN = ("x", "zh", "y", "core")
F32, BF16 = jnp.float32, jnp.bfloat16
UNITS, FEATS, STEP = 832, 2048, 256
PLAIN = (((1,), (0,)), ((), ()))
BY_ROWS = (((1,), (1,)), ((), ()))
BY_COLUMNS = (((0,), (0,)), ((), ()))
SMEM = pl.BlockSpec(memory_space=pltpu.SMEM)
VMEM = pl.BlockSpec(memory_space=pltpu.VMEM)


def swap(value, axis, mask):
    size = lax.axis_size(axis)
    return lax.ppermute(value, axis, [(i, i ^ mask) for i in range(size)])


def gather_over(value, axis):
    return [value] + [swap(value, axis, k) for k in range(1, lax.axis_size(axis))]


def after(values, others):
    return lax.optimization_barrier((values, others))[0]


def dot(left, right, how):
    return lax.dot_general(left, right, how, preferred_element_type=F32)


def one_hot(rows, columns, source):
    row = lax.broadcasted_iota(jnp.int32, (rows, columns), 0)
    column = lax.broadcasted_iota(jnp.int32, (rows, columns), 1)
    return (column == source(row)).astype(F32).astype(BF16)


def prep_kernel(place, gate, up, gate_scale, up_scale, gate_lift, up_lift, both, back_other, back_own):
    zh, core = place[0], place[1]

    def source(row):
        half, side = 1 - row // 64, 1 - row // 32 % 2
        return (half ^ zh) * 64 + row // 8 % 4 * 16 + (side ^ core) * 8 + row % 8

    order = one_hot(128, 128, source)
    none = jnp.zeros((16, UNITS), F32)
    lifts = (
        jnp.concatenate([gate_lift[...], none], 0).astype(BF16),
        jnp.concatenate([none, up_lift[...]], 0).astype(BF16),
    )
    back = jnp.zeros((128, 32), F32)
    for k, (grad, scale) in enumerate(((gate, gate_scale), (up, up_scale))):
        rows = dot(order, grad[...], BY_ROWS)
        back += dot(rows.astype(BF16), lifts[k], BY_ROWS)
        rows = (rows * scale[...].reshape(1, UNITS)).astype(BF16).reshape(2, 2, 32, UNITS)
        both[0, k] = rows[0]
        both[1, k] = rows[1]
    back = back.reshape(2, 2, 32, 32)
    back_other[...] = back[:, 0].reshape(64, 32)
    back_own[...] = back[:, 1].reshape(64, 32)


def prep(place, *arrays):
    both = jax.ShapeDtypeStruct((2, 2, 2, 32, UNITS), BF16)
    back = jax.ShapeDtypeStruct((64, 32), F32)
    return pl.pallas_call(
        prep_kernel,
        out_shape=(both, back, back),
        in_specs=[SMEM] + [VMEM] * 6,
        out_specs=(VMEM,) * 3,
        compiler_params=pltpu.CompilerParams(vmem_limit_bytes=6 << 20),
        cost_estimate=pl.CostEstimate(flops=14_000_000, bytes_accessed=1_200_000, transcendentals=0),
        name="prep",
    )(place, *arrays)


def product_kernel(pairs, *refs):
    blocks, (gate_codes, up_codes, other, own, grads) = refs[:-5], refs[-5:]
    count = len(blocks) // pairs
    for k in range(2):
        for c in range(2):
            for half in range(2):
                for j in range(count):
                    value = blocks[j * pairs][half, k, c]
                    if pairs == 2:
                        value += blocks[j * pairs + 1][half, k, c]
                    row = ((c * 2 + half) * count + j) * 32
                    grads[k, row : row + 32] = value
    gate, up, cut = grads[0], grads[1], 64 * count
    for start in range(0, FEATS, STEP):
        columns = slice(start, start + STEP)
        total = dot(gate, gate_codes[:, columns], PLAIN) + dot(up, up_codes[:, columns], PLAIN)
        other[:, columns] = total[:cut].astype(BF16)
        own[:, columns] = total[cut:].astype(BF16)


def product(blocks, pairs, gate_codes, up_codes):
    count = len(blocks) // pairs
    part = jax.ShapeDtypeStruct((64 * count, FEATS), BF16)
    return pl.pallas_call(
        functools.partial(product_kernel, pairs),
        out_shape=(part, part, jax.ShapeDtypeStruct((2, 128 * count, UNITS), BF16)),
        in_specs=[VMEM] * (len(blocks) + 2),
        out_specs=(VMEM,) * 3,
        compiler_params=pltpu.CompilerParams(vmem_limit_bytes=24 << 20),
        cost_estimate=pl.CostEstimate(
            flops=900_000_000 * count, bytes_accessed=8_000_000, transcendentals=0
        ),
        name="product",
    )(*blocks, gate_codes, up_codes)


def pairs_kernel(place, own1, theirs1, own2, theirs2, far, near):
    for half, out in enumerate((far, near)):
        for j in range(4):
            own, theirs, row = (own1, theirs1, (half * 3 + j) * 32) if j < 3 else (own2, theirs2, half * 32)
            rows = slice(row, row + 32)
            total = own[rows].astype(F32) + theirs[rows].astype(F32)
            out[place[2] ^ j] = total.astype(BF16)


def add_pairs(*arrays):
    out = jax.ShapeDtypeStruct((4, 32, FEATS), BF16)
    return pl.pallas_call(
        pairs_kernel,
        out_shape=(out, out),
        in_specs=[SMEM] + [VMEM] * 4,
        out_specs=(VMEM, VMEM),
        compiler_params=pltpu.CompilerParams(vmem_limit_bytes=8 << 20),
        cost_estimate=pl.CostEstimate(flops=600_000, bytes_accessed=3_200_000, transcendentals=0),
        name="add_pairs",
    )(*arrays)


def spread_kernel(inputs, back, arrived, out):
    tokens = jnp.concatenate([inputs[...].astype(F32), arrived[:, :FEATS].astype(F32)], 0)
    theirs = arrived[:, FEATS:].astype(F32)
    back = back[...] + jnp.concatenate([theirs[4:], theirs[:4]], 0)
    back = jnp.concatenate([back, jnp.zeros((8, 256), F32)], 0)
    for i in range(16):
        out[i, :, :FEATS] = tokens.astype(BF16)
        out[i, :, FEATS:] = back.astype(BF16)


def spread(*arrays):
    return pl.pallas_call(
        spread_kernel,
        out_shape=jax.ShapeDtypeStruct((16, 16, FEATS + 256), BF16),
        in_specs=[VMEM] * 3,
        out_specs=VMEM,
        compiler_params=pltpu.CompilerParams(vmem_limit_bytes=6 << 20),
        cost_estimate=pl.CostEstimate(flops=100_000, bytes_accessed=1_300_000, transcendentals=0),
        name="spread",
    )(*arrays)


def narrow_kernel(landed, gate_down, up_down, out):
    down = jnp.concatenate([gate_down[...], up_down[...]], 0).astype(BF16)
    low = dot(down, landed[:, :, :FEATS].reshape(256, FEATS), BY_ROWS)
    back = jnp.zeros((16, 256), F32)
    for i in range(16):
        back += landed[i, :, FEATS:].astype(F32)
    out[...] = jnp.concatenate([low, back], 0).astype(BF16)


def narrow(*arrays):
    return pl.pallas_call(
        narrow_kernel,
        out_shape=jax.ShapeDtypeStruct((48, 256), BF16),
        in_specs=[VMEM] * 3,
        out_specs=VMEM,
        compiler_params=pltpu.CompilerParams(vmem_limit_bytes=8 << 20),
        cost_estimate=pl.CostEstimate(flops=34_000_000, bytes_accessed=1_500_000, transcendentals=0),
        name="narrow",
    )(*arrays)


def joined_kernel(place, p0, p1, p2, p3, landed, gate_down, up_down, low_out, adapter, reducer):
    hid, x, y = place[2], place[3], place[4]
    parts = [part[...].astype(F32) for part in (p0, p1, p2, p3)]
    low_out[...] = sum(part[:32] for part in parts).astype(BF16)
    back = jnp.concatenate(
        [part[32:40, 32 * i : 32 * i + 32] for part in parts for i in range(8)], 0
    ).astype(BF16)

    def source(row):
        return ((row // 64) ^ hid) * 64 + row % 8 * 8 + (1 - row // 8 % 2) * 4 + row // 16 % 4

    mine = dot(one_hot(16, 256, lambda row: source(x * 64 + y * 16 + row)), back, PLAIN)
    back = (ADAPTER_SCALE * dot(one_hot(256, 256, source), back, PLAIN)).astype(BF16)
    down = jnp.concatenate([gate_down[...], up_down[...]], 0).astype(BF16)
    adapter[...] = ADAPTER_SCALE * dot(mine.astype(BF16), down, PLAIN)[:8]
    reducer[...] = dot(back, landed[:, :, :FEATS].reshape(256, FEATS), BY_COLUMNS)


def joined(place, parts, *arrays):
    return pl.pallas_call(
        joined_kernel,
        out_shape=(
            jax.ShapeDtypeStruct((32, 256), BF16),
            jax.ShapeDtypeStruct((8, FEATS), F32),
            jax.ShapeDtypeStruct((32, FEATS), F32),
        ),
        in_specs=[SMEM] + [VMEM] * 7,
        out_specs=(VMEM,) * 3,
        compiler_params=pltpu.CompilerParams(vmem_limit_bytes=8 << 20),
        cost_estimate=pl.CostEstimate(flops=40_000_000, bytes_accessed=1_700_000, transcendentals=0),
        name="joined",
    )(place, *parts, *arrays)


def expander_kernel(place, low_other, low_own, grads1, grads2, gate_scale, up_scale, gate_out, up_out):
    hid = place[2]
    low = jnp.concatenate([low_other[...], low_own[...]], 1)

    def order(blocks):
        pieces = [
            one_hot(
                32 * len(blocks),
                512,
                lambda row: c * 256 + ((row // 32 + blocks[0]) ^ hid) * 64 + row // 8 % 4 * 16 + (1 - half) * 8 + row % 8,
            )
            for c in range(2)
            for half in range(2)
        ]
        return jnp.concatenate(pieces, 0)

    low1 = dot(low, order((0, 1, 2)), BY_ROWS).astype(BF16)
    low2 = dot(low, order((3,)), BY_ROWS).astype(BF16)
    for k, (out, scale) in enumerate(((gate_out, gate_scale), (up_out, up_scale))):
        total = dot(low1, grads1[k], PLAIN) + dot(low2, grads2[k], PLAIN)
        out[...] = ADAPTER_SCALE * total[16 * k : 16 * k + 16] / scale[...].reshape(1, UNITS)


def expander(*arrays):
    out = jax.ShapeDtypeStruct((16, UNITS), F32)
    return pl.pallas_call(
        expander_kernel,
        out_shape=(out, out),
        in_specs=[SMEM] + [VMEM] * 6,
        out_specs=(VMEM, VMEM),
        compiler_params=pltpu.CompilerParams(vmem_limit_bytes=12 << 20),
        cost_estimate=pl.CostEstimate(flops=55_000_000, bytes_accessed=2_000_000, transcendentals=0),
        name="expander",
    )(*arrays)


def plane(value):
    return lax.all_to_all(value, ("x", "y"), split_axis=0, concat_axis=0, tiled=True)


def per_device(
    inputs, gate_grad, up_grad, gate_codes, up_codes, gate_scale, up_scale,
    gate_down, gate_lift, up_down, up_lift,
):
    hid = lax.axis_index("hid")
    x, zh, y, core = (lax.axis_index(name) for name in FFN)
    place = jnp.stack([zh, core, hid, x, y])
    downs = gate_down.T, up_down.T

    both, back_other, back_own = prep(
        place, gate_grad.T, up_grad.T, gate_scale, up_scale, gate_lift, up_lift
    )
    two, one = swap(both, "hid", 2), swap(both, "hid", 1)
    back = (back_own + swap(back_other, "core", 1)).reshape(8, 256)
    arrived = swap(jnp.concatenate([inputs, back.astype(BF16)], 1), "zh", 1)
    sent, relayed = after((both, two), (one, arrived))
    middle = lax.ppermute(sent, "hid", [(1, 2), (2, 1)])
    ends = lax.ppermute(relayed, "hid", [(1, 0), (2, 3)])

    landed = plane(spread(inputs, back, arrived))
    parts = gather_over(narrow(landed, *downs), "hid")
    low, adapter, reducer = joined(place, parts, landed, *downs)
    reducer = reducer + swap(reducer, "core", 1)
    low_other = swap(low, "core", 1)

    codes = gate_codes.T, up_codes.T
    other1, own1, grads1 = product((both, one, two), 1, *codes)
    other2, own2, grads2 = product((middle, ends), 2, *codes)
    other1 = after(other1, (middle, ends))
    sums = add_pairs(place, own1, swap(other1, "core", 1), own2, swap(other2, "core", 1))
    kept = [plane(half.reshape(16, 8, FEATS)).astype(F32).sum(0) for half in sums]
    gate_expander, up_expander = expander(
        place, low_other, low, grads1, grads2, gate_scale, up_scale
    )
    arrived = swap(kept[0].astype(BF16), "zh", 1)
    rows = (kept[1] + arrived.astype(F32) + adapter).astype(BF16)
    return rows, reducer[:16].T, gate_expander, reducer[16:].T, up_expander


def solution(mesh):
    whole = Mesh(mesh.devices.reshape(4, 4, 2, 4, 2), ("hid",) + FFN)
    placed = (
        P(FFN, "hid"), P("hid", FFN), P("hid", FFN), P("hid", FFN), P("hid", FFN),
        P(FFN), P(FFN), P("hid", None), P(None, FFN), P("hid", None), P(None, FFN),
    )
    return jax.shard_map(
        per_device,
        mesh=whole,
        in_specs=placed,
        out_specs=(P(FFN, "hid"), P("hid", None), P(None, FFN), P("hid", None), P(None, FFN)),
        check_vma=False,
    )
```

```python
import functools

import jax
import jax.numpy as jnp
from jax import lax
from jax.experimental import pallas as pl
from jax.experimental.pallas import tpu as pltpu
from jax.sharding import Mesh, PartitionSpec as P

ADAPTER_SCALE = 2.0
FFN = ("x", "zh", "y", "core")
F32, BF16 = jnp.float32, jnp.bfloat16
UNITS, FEATS, STEP = 832, 2048, 256
PLAIN = (((1,), (0,)), ((), ()))
BY_ROWS = (((1,), (1,)), ((), ()))
BY_COLUMNS = (((0,), (0,)), ((), ()))
SMEM = pl.BlockSpec(memory_space=pltpu.SMEM)
VMEM = pl.BlockSpec(memory_space=pltpu.VMEM)


def swap(value, axis, mask):
    size = lax.axis_size(axis)
    return lax.ppermute(value, axis, [(i, i ^ mask) for i in range(size)])


def gather_over(value, axis):
    return [value] + [swap(value, axis, k) for k in range(1, lax.axis_size(axis))]


def dot(left, right, how):
    return lax.dot_general(left, right, how, preferred_element_type=F32)


def one_hot(rows, columns, source):
    row = lax.broadcasted_iota(jnp.int32, (rows, columns), 0)
    column = lax.broadcasted_iota(jnp.int32, (rows, columns), 1)
    return (column == source(row)).astype(F32).astype(BF16)


def prep_kernel(place, gate, up, gate_scale, up_scale, gate_lift, up_lift, both, back_other, back_own):
    zh, core = place[0], place[1]

    def source(row):
        half, side = 1 - row // 64, 1 - row // 32 % 2
        return (half ^ zh) * 64 + row // 8 % 4 * 16 + (side ^ core) * 8 + row % 8

    order = one_hot(128, 128, source)
    none = jnp.zeros((16, UNITS), F32)
    lifts = (
        jnp.concatenate([gate_lift[...], none], 0).astype(BF16),
        jnp.concatenate([none, up_lift[...]], 0).astype(BF16),
    )
    back = jnp.zeros((128, 32), F32)
    for k, (grad, scale) in enumerate(((gate, gate_scale), (up, up_scale))):
        rows = dot(order, grad[...], BY_ROWS)
        back += dot(rows.astype(BF16), lifts[k], BY_ROWS)
        rows = (rows * scale[...].reshape(1, UNITS)).astype(BF16).reshape(2, 2, 32, UNITS)
        both[0, k] = rows[0]
        both[1, k] = rows[1]

    def packed(row):
        return row // 4 % 2 * 64 + row // 8 % 2 * 32 + row % 4 * 8 + row // 16

    back = dot(one_hot(128, 128, packed), back.astype(BF16), PLAIN)
    back_other[...] = jnp.concatenate([back[16 * i : 16 * i + 8] for i in range(8)], 1)
    back_own[...] = jnp.concatenate([back[16 * i + 8 : 16 * i + 16] for i in range(8)], 1)


def prep(place, *arrays):
    both = jax.ShapeDtypeStruct((2, 2, 2, 32, UNITS), BF16)
    back = jax.ShapeDtypeStruct((8, 256), F32)
    return pl.pallas_call(
        prep_kernel,
        out_shape=(both, back, back),
        in_specs=[SMEM] + [VMEM] * 6,
        out_specs=(VMEM,) * 3,
        cost_estimate=pl.CostEstimate(flops=14_000_000, bytes_accessed=1_200_000, transcendentals=0),
        name="prep",
    )(place, *arrays)


def product_kernel(pairs, *refs):
    blocks, (gate_codes, up_codes, other, own, grads, gate_held, up_held, sems) = refs[:-8], refs[-8:]
    count = len(blocks) // pairs
    copies = []
    for i, start in enumerate(range(0, FEATS, STEP)):
        columns = pl.ds(start, STEP)
        copies.append(
            [
                pltpu.make_async_copy(source.at[:, columns], held.at[:, columns], sems.at[k, i])
                for k, (source, held) in enumerate(((gate_codes, gate_held), (up_codes, up_held)))
            ]
        )
        for copy in copies[-1]:
            copy.start()
    for k in range(2):
        for c in range(2):
            for half in range(2):
                for j in range(count):
                    value = blocks[j * pairs][half, k, c]
                    if pairs == 2:
                        value += blocks[j * pairs + 1][half, k, c]
                    row = ((c * 2 + half) * count + j) * 32
                    grads[k, row : row + 32] = value
    gate, up, cut = grads[0], grads[1], 64 * count
    for i, start in enumerate(range(0, FEATS, STEP)):
        columns = slice(start, start + STEP)
        for copy in copies[i]:
            copy.wait()
        total = dot(gate, gate_held[:, columns], PLAIN) + dot(up, up_held[:, columns], PLAIN)
        other[:, columns] = total[:cut].astype(BF16)
        own[:, columns] = total[cut:].astype(BF16)


def product(blocks, pairs, gate_codes, up_codes):
    count = len(blocks) // pairs
    part = jax.ShapeDtypeStruct((64 * count, FEATS), BF16)
    anywhere = pl.BlockSpec(memory_space=pl.ANY)
    return pl.pallas_call(
        functools.partial(product_kernel, pairs),
        out_shape=(part, part, jax.ShapeDtypeStruct((2, 128 * count, UNITS), BF16)),
        in_specs=[VMEM] * len(blocks) + [anywhere] * 2,
        out_specs=(VMEM,) * 3,
        scratch_shapes=[
            pltpu.VMEM((UNITS, FEATS), BF16),
            pltpu.VMEM((UNITS, FEATS), BF16),
            pltpu.SemaphoreType.DMA((2, FEATS // STEP)),
        ],
        compiler_params=pltpu.CompilerParams(vmem_limit_bytes=20 << 20),
        cost_estimate=pl.CostEstimate(
            flops=900_000_000 * count, bytes_accessed=8_000_000, transcendentals=0
        ),
        name="product",
    )(*blocks, gate_codes, up_codes)


def pairs_kernel(place, own1, theirs1, own2, theirs2, out):
    for j in range(4):
        halves = []
        for half in range(2):
            own, theirs, row = (own1, theirs1, (half * 3 + j) * 32) if j < 3 else (own2, theirs2, half * 32)
            rows = slice(row, row + 32)
            halves.append(own[rows].astype(F32) + theirs[rows].astype(F32))
        for k in range(4):
            rows = slice(8 * k, 8 * k + 8)
            out[place[2] ^ j, k] = jnp.concatenate([half[rows] for half in halves], 0).astype(BF16)


def add_pairs(*arrays):
    return pl.pallas_call(
        pairs_kernel,
        out_shape=jax.ShapeDtypeStruct((4, 4, 16, FEATS), BF16),
        in_specs=[SMEM] + [VMEM] * 4,
        out_specs=VMEM,
        compiler_params=pltpu.CompilerParams(vmem_limit_bytes=8 << 20),
        cost_estimate=pl.CostEstimate(flops=600_000, bytes_accessed=3_200_000, transcendentals=0),
        name="add_pairs",
    )(*arrays)


def mark_kernel(one, two, out):
    out[...] = jnp.zeros((8, 128), F32)


def mark(*arrays):
    return pl.pallas_call(
        mark_kernel,
        out_shape=jax.ShapeDtypeStruct((8, 128), F32),
        in_specs=[pl.BlockSpec(memory_space=pl.ANY)] * 2,
        out_specs=VMEM,
        compiler_params=pltpu.CompilerParams(vmem_limit_bytes=1 << 20),
        cost_estimate=pl.CostEstimate(flops=100_000_000_000, bytes_accessed=4096, transcendentals=0),
        name="mark",
    )(*arrays)


def spread_kernel(inputs, back_own, back_theirs, out):
    rows = jnp.concatenate([inputs[...].astype(F32), back_own[...] + back_theirs[...]], 1)
    rows = jnp.concatenate([rows, rows], 0).astype(BF16)
    for i in range(8):
        out[16 * i : 16 * i + 16] = rows


def spread(*arrays):
    return pl.pallas_call(
        spread_kernel,
        out_shape=jax.ShapeDtypeStruct((128, FEATS + 256), BF16),
        in_specs=[VMEM] * 3,
        out_specs=VMEM,
        compiler_params=pltpu.CompilerParams(vmem_limit_bytes=4 << 20),
        cost_estimate=pl.CostEstimate(flops=40_000_000_000, bytes_accessed=700_000, transcendentals=0),
        name="spread",
    )(*arrays)


def narrow_kernel(marked, landed, gate_down, up_down, out):
    down = jnp.concatenate([gate_down[...], up_down[...]], 0).astype(BF16)
    low = dot(down, landed[:, :FEATS], BY_ROWS)
    back = landed[:, FEATS:].astype(F32).reshape(16, 8, 256).sum(0)
    low = jnp.concatenate([low, jnp.zeros((32, 128), F32)], 1)
    out[...] = jnp.concatenate([low, back, jnp.zeros((8, 256), F32)], 0).astype(BF16)


def narrow(*arrays):
    return pl.pallas_call(
        narrow_kernel,
        out_shape=jax.ShapeDtypeStruct((48, 256), BF16),
        in_specs=[pl.BlockSpec(memory_space=pl.ANY)] + [VMEM] * 3,
        out_specs=VMEM,
        compiler_params=pltpu.CompilerParams(vmem_limit_bytes=6 << 20),
        cost_estimate=pl.CostEstimate(flops=17_000_000, bytes_accessed=900_000, transcendentals=0),
        name="narrow",
    )(*arrays)


def halves_kernel(own, theirs, out):
    mine, other = own[...].astype(F32), theirs[...].astype(F32)
    low = jnp.concatenate([mine[:32, :128], other[:32, :128]], 1)
    back = mine[32:40] + jnp.concatenate([other[36:40], other[32:36]], 0)
    out[...] = jnp.concatenate([low, back, jnp.zeros((8, 256), F32)], 0).astype(BF16)


def join_halves(*arrays):
    return pl.pallas_call(
        halves_kernel,
        out_shape=jax.ShapeDtypeStruct((48, 256), BF16),
        in_specs=[VMEM] * 2,
        out_specs=VMEM,
        compiler_params=pltpu.CompilerParams(vmem_limit_bytes=2 << 20),
        cost_estimate=pl.CostEstimate(flops=10_000, bytes_accessed=80_000, transcendentals=0),
        name="join_halves",
    )(*arrays)


def joined_kernel(marked, place, p0, p1, p2, p3, landed, gate_down, up_down, low_out, adapter, keep, give):
    core, hid, x, y = place[1], place[2], place[3], place[4]
    parts = [part[...].astype(F32) for part in (p0, p1, p2, p3)]
    low_out[...] = sum(part[:32] for part in parts).astype(BF16)
    back = jnp.concatenate(
        [part[32:40, 32 * i : 32 * i + 32] for part in parts for i in range(8)], 0
    ).astype(BF16)

    def source(row):
        return ((row // 32) ^ hid) * 64 + row % 8 * 8 + 4 + row // 8 % 4

    mine = dot(one_hot(16, 256, lambda row: source(x * 32 + y * 8 + row % 8)), back, PLAIN)
    back = (ADAPTER_SCALE * dot(one_hot(128, 256, source), back, PLAIN)).astype(BF16)
    down = jnp.concatenate([gate_down[...], up_down[...]], 0).astype(BF16)
    adapter[...] = ADAPTER_SCALE * dot(mine.astype(BF16), down, PLAIN)[:8]
    reducer = dot(back, landed[:, :FEATS], BY_COLUMNS)
    keep[...] = jnp.where(core == 0, reducer[:16], reducer[16:])
    give[...] = jnp.where(core == 0, reducer[16:], reducer[:16])


def joined(marked, place, parts, *arrays):
    half = jax.ShapeDtypeStruct((16, FEATS), F32)
    return pl.pallas_call(
        joined_kernel,
        out_shape=(
            jax.ShapeDtypeStruct((32, 256), BF16),
            jax.ShapeDtypeStruct((8, FEATS), F32),
            half,
            half,
        ),
        in_specs=[pl.BlockSpec(memory_space=pl.ANY), SMEM] + [VMEM] * 7,
        out_specs=(VMEM,) * 4,
        compiler_params=pltpu.CompilerParams(vmem_limit_bytes=6 << 20),
        cost_estimate=pl.CostEstimate(flops=100_000_000_000, bytes_accessed=1_000_000, transcendentals=0),
        name="joined",
    )(marked, place, *parts, *arrays)


def expander_kernel(place, low_other, low_own, grads1, grads2, gate_scale, up_scale, gate_out, up_out):
    hid = place[2]
    low = jnp.concatenate([low_other[...], low_own[...]], 1)

    def order(blocks):
        pieces = [
            one_hot(
                32 * len(blocks),
                512,
                lambda row: c * 256 + (1 - half) * 128 + ((row // 32 + blocks[0]) ^ hid) * 32 + row % 32,
            )
            for c in range(2)
            for half in range(2)
        ]
        return jnp.concatenate(pieces, 0)

    low1 = dot(low, order((0, 1, 2)), BY_ROWS).astype(BF16)
    low2 = dot(low, order((3,)), BY_ROWS).astype(BF16)
    for k, (out, scale) in enumerate(((gate_out, gate_scale), (up_out, up_scale))):
        total = dot(low1, grads1[k], PLAIN) + dot(low2, grads2[k], PLAIN)
        out[...] = ADAPTER_SCALE * total[16 * k : 16 * k + 16] / scale[...].reshape(1, UNITS)


def expander(*arrays):
    out = jax.ShapeDtypeStruct((16, UNITS), F32)
    return pl.pallas_call(
        expander_kernel,
        out_shape=(out, out),
        in_specs=[SMEM] + [VMEM] * 6,
        out_specs=(VMEM, VMEM),
        compiler_params=pltpu.CompilerParams(vmem_limit_bytes=8 << 20),
        cost_estimate=pl.CostEstimate(flops=55_000_000, bytes_accessed=2_000_000, transcendentals=0),
        name="expander",
    )(*arrays)


def plane(value):
    return lax.all_to_all(value, ("x", "y"), split_axis=0, concat_axis=0, tiled=True)


def per_device(
    inputs, gate_grad, up_grad, gate_codes, up_codes, gate_scale, up_scale,
    gate_down, gate_lift, up_down, up_lift,
):
    hid = lax.axis_index("hid")
    x, zh, y, core = (lax.axis_index(name) for name in FFN)
    place = jnp.stack([zh, core, hid, x, y])
    downs = gate_down.T, up_down.T

    both, back_other, back_own = prep(
        place, gate_grad.T, up_grad.T, gate_scale, up_scale, gate_lift, up_lift
    )
    two, one = swap(both, "hid", 2), swap(both, "hid", 1)
    gathered = spread(inputs, back_own, swap(back_other, "core", 1))

    landed = plane(gathered)
    both, two, one, landed, marked = lax.optimization_barrier(
        (both, two, one, landed, mark(one, two))
    )
    middle = lax.ppermute(both, "hid", [(1, 2), (2, 1)])
    ends = lax.ppermute(two, "hid", [(1, 0), (2, 3)])

    codes = gate_codes.T, up_codes.T
    small = narrow(marked, landed, *downs)
    small_theirs = swap(small, "zh", 1)
    other1, own1, grads1 = product((both, one, two), 1, *codes)
    other1, middle, ends, marked = lax.optimization_barrier(
        (other1, middle, ends, mark(middle, ends))
    )
    other2, own2, grads2 = product((middle, ends), 2, *codes)
    sums = add_pairs(place, own1, swap(other1, "core", 1), own2, swap(other2, "core", 1))
    kept = plane(sums.reshape(256, FEATS)).astype(F32).reshape(16, 16, FEATS).sum(0)

    small = join_halves(small, small_theirs)
    low, adapter, keep, give = joined(marked, place, gather_over(small, "hid"), landed, *downs)
    low_other = swap(low, "core", 1)
    half = (keep + swap(give, "core", 1)).astype(BF16)
    mine = half.astype(F32) + swap(half, "zh", 1).astype(F32)
    theirs = swap(mine, "core", 1)
    gate_reducer, up_reducer = (jnp.where(core == k, mine, theirs) for k in range(2))
    gate_expander, up_expander = expander(
        place, low_other, low, grads1, grads2, gate_scale, up_scale
    )
    arrived = swap(kept[:8].astype(BF16), "zh", 1)
    rows = (kept[8:] + arrived.astype(F32) + adapter).astype(BF16)
    return rows, gate_reducer.T, gate_expander, up_reducer.T, up_expander


def solution(mesh):
    whole = Mesh(mesh.devices.reshape(4, 4, 2, 4, 2), ("hid",) + FFN)
    placed = (
        P(FFN, "hid"), P("hid", FFN), P("hid", FFN), P("hid", FFN), P("hid", FFN),
        P(FFN), P(FFN), P("hid", None), P(None, FFN), P("hid", None), P(None, FFN),
    )
    return jax.shard_map(
        per_device,
        mesh=whole,
        in_specs=placed,
        out_specs=(P(FFN, "hid"), P("hid", None), P(None, FFN), P("hid", None), P(None, FFN)),
        check_vma=False,
    )
```

```python
import functools

import jax
import jax.numpy as jnp
from jax import lax
from jax.experimental import pallas as pl
from jax.experimental.pallas import tpu as pltpu
from jax.sharding import Mesh, PartitionSpec as P

ADAPTER_SCALE = 2.0
FFN = ("x", "zh", "y", "core")
F32, BF16 = jnp.float32, jnp.bfloat16
UNITS, FEATS, STEP, CHUNK = 832, 2048, 256, 512
PLAIN = (((1,), (0,)), ((), ()))
BY_ROWS = (((1,), (1,)), ((), ()))
BY_COLUMNS = (((0,), (0,)), ((), ()))
SMEM = pl.BlockSpec(memory_space=pltpu.SMEM)
VMEM = pl.BlockSpec(memory_space=pltpu.VMEM)


def swap(value, axis, mask):
    size = lax.axis_size(axis)
    return lax.ppermute(value, axis, [(i, i ^ mask) for i in range(size)])


def swap_each(values, axis):
    return [swap(value, axis, k) if k else value for k, value in enumerate(values)]


def gather_over(value, axis):
    return [value] + [swap(value, axis, k) for k in range(1, lax.axis_size(axis))]


def dot(left, right, how):
    return lax.dot_general(left, right, how, preferred_element_type=F32)


def one_hot(rows, columns, source):
    row = lax.broadcasted_iota(jnp.int32, (rows, columns), 0)
    column = lax.broadcasted_iota(jnp.int32, (rows, columns), 1)
    return (column == source(row)).astype(F32).astype(BF16)


def prep_kernel(place, gate, up, gate_scale, up_scale, gate_lift, up_lift, both, back_other, back_own):
    zh, core = place[0], place[1]

    def source(row):
        half, side = 1 - row // 64, 1 - row // 32 % 2
        return (half ^ zh) * 64 + row // 8 % 4 * 16 + (side ^ core) * 8 + row % 8

    order = one_hot(128, 128, source)
    none = jnp.zeros((16, UNITS), F32)
    lifts = (
        jnp.concatenate([gate_lift[...], none], 0).astype(BF16),
        jnp.concatenate([none, up_lift[...]], 0).astype(BF16),
    )
    back = jnp.zeros((128, 32), F32)
    for k, (grad, scale) in enumerate(((gate, gate_scale), (up, up_scale))):
        rows = dot(order, grad[...], BY_ROWS)
        back += dot(rows.astype(BF16), lifts[k], BY_ROWS)
        rows = (rows * scale[...].reshape(1, UNITS)).astype(BF16).reshape(2, 2, 32, UNITS)
        both[0, k] = rows[0]
        both[1, k] = rows[1]

    def packed(row):
        return row // 4 % 2 * 64 + row // 8 % 2 * 32 + row % 4 * 8 + row // 16

    back = dot(one_hot(128, 128, packed), back.astype(BF16), PLAIN)
    back_other[...] = jnp.concatenate([back[16 * i : 16 * i + 8] for i in range(8)], 1)
    back_own[...] = jnp.concatenate([back[16 * i + 8 : 16 * i + 16] for i in range(8)], 1)


def prep(place, *arrays):
    both = jax.ShapeDtypeStruct((2, 2, 2, 32, UNITS), BF16)
    back = jax.ShapeDtypeStruct((8, 256), F32)
    return pl.pallas_call(
        prep_kernel,
        out_shape=(both, back, back),
        in_specs=[SMEM] + [VMEM] * 6,
        out_specs=(VMEM,) * 3,
        cost_estimate=pl.CostEstimate(flops=14_000_000, bytes_accessed=1_200_000, transcendentals=0),
        name="prep",
    )(place, *arrays)


def product_kernel(pairs, *refs):
    blocks, (gate_codes, up_codes, other, own, grads, gate_held, up_held, sems) = refs[:-8], refs[-8:]
    count = len(blocks) // pairs
    def copies(i):
        columns = pl.ds(i * CHUNK, CHUNK)
        return [
            pltpu.make_async_copy(source.at[:, columns], held.at[:, columns], sems.at[k, i])
            for k, (source, held) in enumerate(((gate_codes, gate_held), (up_codes, up_held)))
        ]

    for copy in copies(0) + copies(1):
        copy.start()
    for k in range(2):
        for c in range(2):
            for half in range(2):
                for j in range(count):
                    value = blocks[j * pairs][half, k, c]
                    if pairs == 2:
                        value += blocks[j * pairs + 1][half, k, c]
                    row = ((c * 2 + half) * count + j) * 32
                    grads[k, row : row + 32] = value
    gate, up, cut = grads[0], grads[1], 64 * count
    for start in range(0, FEATS, STEP):
        columns = slice(start, start + STEP)
        if start % CHUNK == 0:
            i = start // CHUNK
            for copy in copies(i):
                copy.wait()
            if i + 2 < FEATS // CHUNK:
                for copy in copies(i + 2):
                    copy.start()
        total = dot(gate, gate_held[:, columns], PLAIN) + dot(up, up_held[:, columns], PLAIN)
        other[:, columns] = total[:cut].astype(BF16)
        own[:, columns] = total[cut:].astype(BF16)


def product(blocks, pairs, gate_codes, up_codes):
    count = len(blocks) // pairs
    part = jax.ShapeDtypeStruct((64 * count, FEATS), BF16)
    anywhere = pl.BlockSpec(memory_space=pl.ANY)
    return pl.pallas_call(
        functools.partial(product_kernel, pairs),
        out_shape=(part, part, jax.ShapeDtypeStruct((2, 128 * count, UNITS), BF16)),
        in_specs=[VMEM] * len(blocks) + [anywhere] * 2,
        out_specs=(VMEM,) * 3,
        scratch_shapes=[
            pltpu.VMEM((UNITS, FEATS), BF16),
            pltpu.VMEM((UNITS, FEATS), BF16),
            pltpu.SemaphoreType.DMA((2, FEATS // CHUNK)),
        ],
        compiler_params=pltpu.CompilerParams(vmem_limit_bytes=44 << 20),
        cost_estimate=pl.CostEstimate(
            flops=900_000_000 * count, bytes_accessed=8_000_000, transcendentals=0
        ),
        name="product",
    )(*blocks, gate_codes, up_codes)


def pairs_kernel(place, own1, theirs1, own2, theirs2, *refs):
    outs, sums = refs[:8], refs[8]
    hid_x, y = place[2] ^ place[3], place[4]
    for half in range(2):
        for j in range(4):
            own, theirs, row = (own1, theirs1, (half * 3 + j) * 32) if j < 3 else (own2, theirs2, half * 32)
            rows = slice(row, row + 32)
            sums[half, j] = own[rows].astype(F32) + theirs[rows].astype(F32)
    for k in range(4):
        outs[k][...] = sums[0, hid_x ^ k].astype(BF16)
        rows = pl.ds(pl.multiple_of((y ^ k) * 8, 8), 8)
        outs[4 + k][...] = jnp.concatenate([sums[1, j, rows] for j in range(4)], 0).astype(BF16)


def add_pairs(*arrays):
    return pl.pallas_call(
        pairs_kernel,
        out_shape=(jax.ShapeDtypeStruct((32, FEATS), BF16),) * 8,
        in_specs=[SMEM] + [VMEM] * 4,
        out_specs=(VMEM,) * 8,
        scratch_shapes=[pltpu.VMEM((2, 4, 32, FEATS), F32)],
        compiler_params=pltpu.CompilerParams(vmem_limit_bytes=12 << 20),
        cost_estimate=pl.CostEstimate(flops=600_000, bytes_accessed=3_200_000, transcendentals=0),
        name="add_pairs",
    )(*arrays)


def turn_kernel(place, *refs):
    parts, outs, far, near = refs[:8], refs[8:16], refs[16], refs[17]
    hid_x, y = place[2] ^ place[3], place[4]
    far[...] = sum(part[...].astype(F32) for part in parts[:4])
    near[...] = sum(part[...].astype(F32) for part in parts[4:]).reshape(4, 8, FEATS)
    for k in range(4):
        outs[k][...] = far[pl.ds(pl.multiple_of((y ^ k) * 8, 8), 8)]
        outs[4 + k][...] = near[hid_x ^ k]


def turn(*arrays):
    return pl.pallas_call(
        turn_kernel,
        out_shape=(jax.ShapeDtypeStruct((8, FEATS), F32),) * 8,
        in_specs=[SMEM] + [VMEM] * 8,
        out_specs=(VMEM,) * 8,
        scratch_shapes=[pltpu.VMEM((32, FEATS), F32), pltpu.VMEM((4, 8, FEATS), F32)],
        compiler_params=pltpu.CompilerParams(vmem_limit_bytes=8 << 20),
        cost_estimate=pl.CostEstimate(flops=600_000, bytes_accessed=2_000_000, transcendentals=0),
        name="turn",
    )(*arrays)


def mark_kernel(one, two, out):
    out[...] = jnp.zeros((8, 128), F32)


def mark(*arrays):
    return pl.pallas_call(
        mark_kernel,
        out_shape=jax.ShapeDtypeStruct((8, 128), F32),
        in_specs=[pl.BlockSpec(memory_space=pl.ANY)] * 2,
        out_specs=VMEM,
        compiler_params=pltpu.CompilerParams(vmem_limit_bytes=1 << 20),
        cost_estimate=pl.CostEstimate(flops=100_000_000_000, bytes_accessed=4096, transcendentals=0),
        name="mark",
    )(*arrays)


def spread_kernel(inputs, back_own, back_theirs, out):
    rows = jnp.concatenate([inputs[...].astype(F32), back_own[...] + back_theirs[...]], 1)
    rows = jnp.concatenate([rows, rows], 0).astype(BF16)
    for i in range(8):
        out[16 * i : 16 * i + 16] = rows


def spread(*arrays):
    return pl.pallas_call(
        spread_kernel,
        out_shape=jax.ShapeDtypeStruct((128, FEATS + 256), BF16),
        in_specs=[VMEM] * 3,
        out_specs=VMEM,
        compiler_params=pltpu.CompilerParams(vmem_limit_bytes=4 << 20),
        cost_estimate=pl.CostEstimate(flops=40_000_000_000, bytes_accessed=700_000, transcendentals=0),
        name="spread",
    )(*arrays)


def narrow_kernel(marked, landed, gate_down, up_down, out):
    down = jnp.concatenate([gate_down[...], up_down[...]], 0).astype(BF16)
    low = dot(down, landed[:, :FEATS], BY_ROWS)
    back = landed[:, FEATS:].astype(F32).reshape(16, 8, 256).sum(0)
    low = jnp.concatenate([low, jnp.zeros((32, 128), F32)], 1)
    out[...] = jnp.concatenate([low, back, jnp.zeros((8, 256), F32)], 0).astype(BF16)


def narrow(*arrays):
    return pl.pallas_call(
        narrow_kernel,
        out_shape=jax.ShapeDtypeStruct((48, 256), BF16),
        in_specs=[pl.BlockSpec(memory_space=pl.ANY)] + [VMEM] * 3,
        out_specs=VMEM,
        compiler_params=pltpu.CompilerParams(vmem_limit_bytes=6 << 20),
        cost_estimate=pl.CostEstimate(flops=17_000_000, bytes_accessed=900_000, transcendentals=0),
        name="narrow",
    )(*arrays)


def halves_kernel(own, theirs, out):
    mine, other = own[...].astype(F32), theirs[...].astype(F32)
    low = jnp.concatenate([mine[:32, :128], other[:32, :128]], 1)
    back = mine[32:40] + jnp.concatenate([other[36:40], other[32:36]], 0)
    out[...] = jnp.concatenate([low, back, jnp.zeros((8, 256), F32)], 0).astype(BF16)


def join_halves(*arrays):
    return pl.pallas_call(
        halves_kernel,
        out_shape=jax.ShapeDtypeStruct((48, 256), BF16),
        in_specs=[VMEM] * 2,
        out_specs=VMEM,
        compiler_params=pltpu.CompilerParams(vmem_limit_bytes=2 << 20),
        cost_estimate=pl.CostEstimate(flops=10_000, bytes_accessed=80_000, transcendentals=0),
        name="join_halves",
    )(*arrays)


def joined_kernel(marked, place, p0, p1, p2, p3, landed, gate_down, up_down, low_out, adapter, keep, give):
    core, hid, x, y = place[1], place[2], place[3], place[4]
    parts = [part[...].astype(F32) for part in (p0, p1, p2, p3)]
    low_out[...] = sum(part[:32] for part in parts).astype(BF16)
    back = jnp.concatenate(
        [part[32:40, 32 * i : 32 * i + 32] for part in parts for i in range(8)], 0
    ).astype(BF16)

    def source(row):
        return ((row // 32) ^ hid) * 64 + row % 8 * 8 + 4 + row // 8 % 4

    mine = dot(one_hot(16, 256, lambda row: source(x * 32 + y * 8 + row % 8)), back, PLAIN)
    back = (ADAPTER_SCALE * dot(one_hot(128, 256, source), back, PLAIN)).astype(BF16)
    down = jnp.concatenate([gate_down[...], up_down[...]], 0).astype(BF16)
    adapter[...] = ADAPTER_SCALE * dot(mine.astype(BF16), down, PLAIN)[:8]
    reducer = dot(back, landed[:, :FEATS], BY_COLUMNS)
    keep[...] = jnp.where(core == 0, reducer[:16], reducer[16:])
    give[...] = jnp.where(core == 0, reducer[16:], reducer[:16])


def joined(marked, place, parts, *arrays):
    half = jax.ShapeDtypeStruct((16, FEATS), F32)
    return pl.pallas_call(
        joined_kernel,
        out_shape=(
            jax.ShapeDtypeStruct((32, 256), BF16),
            jax.ShapeDtypeStruct((8, FEATS), F32),
            half,
            half,
        ),
        in_specs=[pl.BlockSpec(memory_space=pl.ANY), SMEM] + [VMEM] * 7,
        out_specs=(VMEM,) * 4,
        compiler_params=pltpu.CompilerParams(vmem_limit_bytes=6 << 20),
        cost_estimate=pl.CostEstimate(flops=100_000_000_000, bytes_accessed=1_000_000, transcendentals=0),
        name="joined",
    )(marked, place, *parts, *arrays)


def expander_kernel(place, low_other, low_own, grads1, grads2, gate_scale, up_scale, gate_out, up_out):
    hid = place[2]
    low = jnp.concatenate([low_other[...], low_own[...]], 1)

    def order(blocks):
        pieces = [
            one_hot(
                32 * len(blocks),
                512,
                lambda row: c * 256 + (1 - half) * 128 + ((row // 32 + blocks[0]) ^ hid) * 32 + row % 32,
            )
            for c in range(2)
            for half in range(2)
        ]
        return jnp.concatenate(pieces, 0)

    low1 = dot(low, order((0, 1, 2)), BY_ROWS).astype(BF16)
    low2 = dot(low, order((3,)), BY_ROWS).astype(BF16)
    for k, (out, scale) in enumerate(((gate_out, gate_scale), (up_out, up_scale))):
        total = dot(low1, grads1[k], PLAIN) + dot(low2, grads2[k], PLAIN)
        out[...] = ADAPTER_SCALE * total[16 * k : 16 * k + 16] / scale[...].reshape(1, UNITS)


def expander(*arrays):
    out = jax.ShapeDtypeStruct((16, UNITS), F32)
    return pl.pallas_call(
        expander_kernel,
        out_shape=(out, out),
        in_specs=[SMEM] + [VMEM] * 6,
        out_specs=(VMEM, VMEM),
        compiler_params=pltpu.CompilerParams(vmem_limit_bytes=8 << 20),
        cost_estimate=pl.CostEstimate(flops=55_000_000, bytes_accessed=2_000_000, transcendentals=0),
        name="expander",
    )(*arrays)


def plane(value):
    return lax.all_to_all(value, ("x", "y"), split_axis=0, concat_axis=0, tiled=True)


def per_device(
    inputs, gate_grad, up_grad, gate_codes, up_codes, gate_scale, up_scale,
    gate_down, gate_lift, up_down, up_lift,
):
    hid = lax.axis_index("hid")
    x, zh, y, core = (lax.axis_index(name) for name in FFN)
    place = jnp.stack([zh, core, hid, x, y])
    downs = gate_down.T, up_down.T

    both, back_other, back_own = prep(
        place, gate_grad.T, up_grad.T, gate_scale, up_scale, gate_lift, up_lift
    )
    two, one = swap(both, "hid", 2), swap(both, "hid", 1)
    gathered = spread(inputs, back_own, swap(back_other, "core", 1))

    landed = plane(gathered)
    both, two, one, landed, marked = lax.optimization_barrier(
        (both, two, one, landed, mark(one, two))
    )
    middle = lax.ppermute(both, "hid", [(1, 2), (2, 1)])
    ends = lax.ppermute(two, "hid", [(1, 0), (2, 3)])

    codes = gate_codes.T, up_codes.T
    small = narrow(marked, landed, *downs)
    small_theirs = swap(small, "zh", 1)
    other1, own1, grads1 = product((both, one, two), 1, *codes)
    other1, middle, ends, marked = lax.optimization_barrier(
        (other1, middle, ends, mark(middle, ends))
    )
    other2, own2, grads2 = product((middle, ends), 2, *codes)
    sums = add_pairs(place, own1, swap(other1, "core", 1), own2, swap(other2, "core", 1))
    sums = turn(place, *swap_each(sums[:4], "x"), *swap_each(sums[4:], "y"))
    kept = sum(swap_each(sums[:4], "y")), sum(swap_each(sums[4:], "x"))

    small = join_halves(small, small_theirs)
    low, adapter, keep, give = joined(marked, place, gather_over(small, "hid"), landed, *downs)
    low_other = swap(low, "core", 1)
    half = (keep + swap(give, "core", 1)).astype(BF16)
    mine = half.astype(F32) + swap(half, "zh", 1).astype(F32)
    theirs = swap(mine, "core", 1)
    gate_reducer, up_reducer = (jnp.where(core == k, mine, theirs) for k in range(2))
    gate_expander, up_expander = expander(
        place, low_other, low, grads1, grads2, gate_scale, up_scale
    )
    arrived = swap(kept[0].astype(BF16), "zh", 1)
    rows = (kept[1] + arrived.astype(F32) + adapter).astype(BF16)
    return rows, gate_reducer.T, gate_expander, up_reducer.T, up_expander


def solution(mesh):
    whole = Mesh(mesh.devices.reshape(4, 4, 2, 4, 2), ("hid",) + FFN)
    placed = (
        P(FFN, "hid"), P("hid", FFN), P("hid", FFN), P("hid", FFN), P("hid", FFN),
        P(FFN), P(FFN), P("hid", None), P(None, FFN), P("hid", None), P(None, FFN),
    )
    return jax.shard_map(
        per_device,
        mesh=whole,
        in_specs=placed,
        out_specs=(P(FFN, "hid"), P("hid", None), P(None, FFN), P("hid", None), P(None, FFN)),
        check_vma=False,
    )
```

```python
import functools

import jax
import jax.numpy as jnp
from jax import lax
from jax.experimental import pallas as pl
from jax.experimental.pallas import tpu as pltpu
from jax.sharding import Mesh, PartitionSpec as P

ADAPTER_SCALE = 2.0
FFN = ("x", "zh", "y", "core")
F32, BF16 = jnp.float32, jnp.bfloat16
UNITS, BOTH, FEATS, STEP, CHUNK = 832, 1664, 2048, 256, 512
PLAIN = (((1,), (0,)), ((), ()))
BY_ROWS = (((1,), (1,)), ((), ()))
BY_COLUMNS = (((0,), (0,)), ((), ()))
SMEM = pl.BlockSpec(memory_space=pltpu.SMEM)
VMEM = pl.BlockSpec(memory_space=pltpu.VMEM)


def swap(value, axis, mask):
    size = lax.axis_size(axis)
    return lax.ppermute(value, axis, [(i, i ^ mask) for i in range(size)])


def gather_over(value, axis):
    return [value] + [swap(value, axis, k) for k in range(1, lax.axis_size(axis))]


def dot(left, right, how):
    return lax.dot_general(left, right, how, preferred_element_type=F32)


def one_hot(rows, columns, source):
    row = lax.broadcasted_iota(jnp.int32, (rows, columns), 0)
    column = lax.broadcasted_iota(jnp.int32, (rows, columns), 1)
    return (column == source(row)).astype(F32).astype(BF16)


def prep_kernel(place, gate, up, gate_scale, up_scale, gate_lift, up_lift, both, back_other, back_own):
    zh, core = place[0], place[1]

    def source(row):
        half, side = 1 - row // 64, 1 - row // 32 % 2
        return (half ^ zh) * 64 + row // 8 % 4 * 16 + (side ^ core) * 8 + row % 8

    order = one_hot(128, 128, source)
    none = jnp.zeros((16, UNITS), F32)
    lifts = (
        jnp.concatenate([gate_lift[...], none], 0).astype(BF16),
        jnp.concatenate([none, up_lift[...]], 0).astype(BF16),
    )
    back, scaled = jnp.zeros((128, 32), F32), []
    for k, (grad, scale) in enumerate(((gate, gate_scale), (up, up_scale))):
        rows = dot(order, grad[...], BY_ROWS)
        back += dot(rows.astype(BF16), lifts[k], BY_ROWS)
        scaled.append(rows * scale[...].reshape(1, UNITS))
    both[...] = jnp.concatenate(scaled, 1).astype(BF16).reshape(2, 2, 32, BOTH)

    def packed(row):
        return row // 4 % 2 * 64 + row // 8 % 2 * 32 + row % 4 * 8 + row // 16

    back = dot(one_hot(128, 128, packed), back.astype(BF16), PLAIN)
    back_other[...] = jnp.concatenate([back[16 * i : 16 * i + 8] for i in range(8)], 1)
    back_own[...] = jnp.concatenate([back[16 * i + 8 : 16 * i + 16] for i in range(8)], 1)


def prep(place, *arrays):
    both = jax.ShapeDtypeStruct((2, 2, 32, BOTH), BF16)
    back = jax.ShapeDtypeStruct((8, 256), F32)
    return pl.pallas_call(
        prep_kernel,
        out_shape=(both, back, back),
        in_specs=[SMEM] + [VMEM] * 6,
        out_specs=(VMEM,) * 3,
        cost_estimate=pl.CostEstimate(flops=14_000_000, bytes_accessed=1_200_000, transcendentals=0),
        name="prep",
    )(place, *arrays)


def product_kernel(pairs, *refs):
    blocks, (gate_codes, up_codes, other, own, grads, held, sems) = refs[:-7], refs[-7:]
    count = len(blocks) // pairs

    def copies(i):
        columns = pl.ds(i * CHUNK, CHUNK)
        return [
            pltpu.make_async_copy(
                source.at[:, columns], held.at[pl.ds(k * UNITS, UNITS), columns], sems.at[k, i]
            )
            for k, source in enumerate((gate_codes, up_codes))
        ]

    for copy in copies(0) + copies(1):
        copy.start()
    for c in range(2):
        for half in range(2):
            for j in range(count):
                value = blocks[j * pairs][half, c]
                if pairs == 2:
                    value += blocks[j * pairs + 1][half, c]
                row = ((c * 2 + half) * count + j) * 32
                grads[row : row + 32] = value
    rows, cut = grads[...], 64 * count
    for start in range(0, FEATS, STEP):
        columns = slice(start, start + STEP)
        if start % CHUNK == 0:
            i = start // CHUNK
            for copy in copies(i):
                copy.wait()
            if i + 2 < FEATS // CHUNK:
                for copy in copies(i + 2):
                    copy.start()
        total = dot(rows, held[:, columns], PLAIN)
        other[:, columns] = total[:cut].astype(BF16)
        own[:, columns] = total[cut:].astype(BF16)


def product(blocks, pairs, gate_codes, up_codes):
    count = len(blocks) // pairs
    part = jax.ShapeDtypeStruct((64 * count, FEATS), BF16)
    anywhere = pl.BlockSpec(memory_space=pl.ANY)
    return pl.pallas_call(
        functools.partial(product_kernel, pairs),
        out_shape=(part, part, jax.ShapeDtypeStruct((128 * count, BOTH), BF16)),
        in_specs=[VMEM] * len(blocks) + [anywhere] * 2,
        out_specs=(VMEM,) * 3,
        scratch_shapes=[
            pltpu.VMEM((BOTH, FEATS), BF16),
            pltpu.SemaphoreType.DMA((2, FEATS // CHUNK)),
        ],
        compiler_params=pltpu.CompilerParams(vmem_limit_bytes=44 << 20),
        cost_estimate=pl.CostEstimate(
            flops=900_000_000 * count, bytes_accessed=8_000_000, transcendentals=0
        ),
        name="product",
    )(*blocks, gate_codes, up_codes)


def pairs_kernel(marked, place, own1, theirs1, own2, theirs2, out):
    for j in range(4):
        halves = []
        for half in range(2):
            own, theirs, row = (own1, theirs1, (half * 3 + j) * 32) if j < 3 else (own2, theirs2, half * 32)
            rows = slice(row, row + 32)
            halves.append(own[rows].astype(F32) + theirs[rows].astype(F32))
        for k in range(4):
            rows = slice(8 * k, 8 * k + 8)
            out[place[2] ^ j, k] = jnp.concatenate([half[rows] for half in halves], 0).astype(BF16)


def add_pairs(*arrays):
    return pl.pallas_call(
        pairs_kernel,
        out_shape=jax.ShapeDtypeStruct((4, 4, 16, FEATS), BF16),
        in_specs=[pl.BlockSpec(memory_space=pl.ANY), SMEM] + [VMEM] * 4,
        out_specs=VMEM,
        compiler_params=pltpu.CompilerParams(vmem_limit_bytes=8 << 20),
        cost_estimate=pl.CostEstimate(flops=600_000, bytes_accessed=3_200_000, transcendentals=0),
        name="add_pairs",
    )(*arrays)


def mark_kernel(*refs):
    refs[-1][...] = jnp.zeros((8, 128), F32)


def mark(*arrays):
    return pl.pallas_call(
        mark_kernel,
        out_shape=jax.ShapeDtypeStruct((8, 128), F32),
        in_specs=[pl.BlockSpec(memory_space=pl.ANY)] * len(arrays),
        out_specs=VMEM,
        compiler_params=pltpu.CompilerParams(vmem_limit_bytes=1 << 20),
        cost_estimate=pl.CostEstimate(flops=100_000_000_000, bytes_accessed=4096, transcendentals=0),
        name="mark",
    )(*arrays)


def spread_kernel(inputs, back_own, back_theirs, out):
    rows = jnp.concatenate([inputs[...].astype(F32), back_own[...] + back_theirs[...]], 1)
    rows = jnp.concatenate([rows, rows], 0).astype(BF16)
    for i in range(8):
        out[16 * i : 16 * i + 16] = rows


def spread(*arrays):
    return pl.pallas_call(
        spread_kernel,
        out_shape=jax.ShapeDtypeStruct((128, FEATS + 256), BF16),
        in_specs=[VMEM] * 3,
        out_specs=VMEM,
        compiler_params=pltpu.CompilerParams(vmem_limit_bytes=4 << 20),
        cost_estimate=pl.CostEstimate(flops=40_000_000_000, bytes_accessed=700_000, transcendentals=0),
        name="spread",
    )(*arrays)


def narrow_kernel(marked, landed, gate_down, up_down, out):
    down = jnp.concatenate([gate_down[...], up_down[...]], 0).astype(BF16)
    low = dot(down, landed[:, :FEATS], BY_ROWS)
    back = landed[:, FEATS:].astype(F32).reshape(16, 8, 256).sum(0)
    low = jnp.concatenate([low, jnp.zeros((32, 128), F32)], 1)
    out[...] = jnp.concatenate([low, back, jnp.zeros((8, 256), F32)], 0).astype(BF16)


def narrow(*arrays):
    return pl.pallas_call(
        narrow_kernel,
        out_shape=jax.ShapeDtypeStruct((48, 256), BF16),
        in_specs=[pl.BlockSpec(memory_space=pl.ANY)] + [VMEM] * 3,
        out_specs=VMEM,
        compiler_params=pltpu.CompilerParams(vmem_limit_bytes=6 << 20),
        cost_estimate=pl.CostEstimate(flops=17_000_000, bytes_accessed=900_000, transcendentals=0),
        name="narrow",
    )(*arrays)


def halves_kernel(own, theirs, out):
    mine, other = own[...].astype(F32), theirs[...].astype(F32)
    low = jnp.concatenate([mine[:32, :128], other[:32, :128]], 1)
    back = mine[32:40] + jnp.concatenate([other[36:40], other[32:36]], 0)
    out[...] = jnp.concatenate([low, back, jnp.zeros((8, 256), F32)], 0).astype(BF16)


def join_halves(*arrays):
    return pl.pallas_call(
        halves_kernel,
        out_shape=jax.ShapeDtypeStruct((48, 256), BF16),
        in_specs=[VMEM] * 2,
        out_specs=VMEM,
        compiler_params=pltpu.CompilerParams(vmem_limit_bytes=2 << 20),
        cost_estimate=pl.CostEstimate(flops=10_000, bytes_accessed=80_000, transcendentals=0),
        name="join_halves",
    )(*arrays)


def joined_kernel(marked, place, p0, p1, p2, p3, landed, gate_down, up_down, low_out, adapter, keep, give):
    core, hid, x, y = place[1], place[2], place[3], place[4]
    parts = [part[...].astype(F32) for part in (p0, p1, p2, p3)]
    low_out[...] = sum(part[:32] for part in parts).astype(BF16)
    back = jnp.concatenate(
        [part[32:40, 32 * i : 32 * i + 32] for part in parts for i in range(8)], 0
    ).astype(BF16)

    def source(row):
        return ((row // 32) ^ hid) * 64 + row % 8 * 8 + 4 + row // 8 % 4

    mine = dot(one_hot(16, 256, lambda row: source(x * 32 + y * 8 + row % 8)), back, PLAIN)
    back = (ADAPTER_SCALE * dot(one_hot(128, 256, source), back, PLAIN)).astype(BF16)
    down = jnp.concatenate([gate_down[...], up_down[...]], 0).astype(BF16)
    adapter[...] = ADAPTER_SCALE * dot(mine.astype(BF16), down, PLAIN)[:8]
    reducer = dot(back, landed[:, :FEATS], BY_COLUMNS)
    keep[...] = jnp.where(core == 0, reducer[:16], reducer[16:])
    give[...] = jnp.where(core == 0, reducer[16:], reducer[:16])


def joined(marked, place, parts, *arrays):
    half = jax.ShapeDtypeStruct((16, FEATS), F32)
    return pl.pallas_call(
        joined_kernel,
        out_shape=(
            jax.ShapeDtypeStruct((32, 256), BF16),
            jax.ShapeDtypeStruct((8, FEATS), F32),
            half,
            half,
        ),
        in_specs=[pl.BlockSpec(memory_space=pl.ANY), SMEM] + [VMEM] * 7,
        out_specs=(VMEM,) * 4,
        compiler_params=pltpu.CompilerParams(vmem_limit_bytes=6 << 20),
        cost_estimate=pl.CostEstimate(flops=100_000_000_000, bytes_accessed=1_000_000, transcendentals=0),
        name="joined",
    )(marked, place, *parts, *arrays)


def expander_kernel(place, low_other, low_own, grads1, grads2, gate_scale, up_scale, gate_out, up_out):
    hid = place[2]
    low = jnp.concatenate([low_other[...], low_own[...]], 1)

    def order(blocks):
        pieces = [
            one_hot(
                32 * len(blocks),
                512,
                lambda row: c * 256 + (1 - half) * 128 + ((row // 32 + blocks[0]) ^ hid) * 32 + row % 32,
            )
            for c in range(2)
            for half in range(2)
        ]
        return jnp.concatenate(pieces, 0)

    low1 = dot(low, order((0, 1, 2)), BY_ROWS).astype(BF16)
    low2 = dot(low, order((3,)), BY_ROWS).astype(BF16)
    total = ADAPTER_SCALE * (dot(low1, grads1[...], PLAIN) + dot(low2, grads2[...], PLAIN))
    gate_out[...] = total[:16, :UNITS] / gate_scale[...].reshape(1, UNITS)
    up_out[...] = total[16:, UNITS:] / up_scale[...].reshape(1, UNITS)


def expander(*arrays):
    out = jax.ShapeDtypeStruct((16, UNITS), F32)
    return pl.pallas_call(
        expander_kernel,
        out_shape=(out, out),
        in_specs=[SMEM] + [VMEM] * 6,
        out_specs=(VMEM, VMEM),
        compiler_params=pltpu.CompilerParams(vmem_limit_bytes=8 << 20),
        cost_estimate=pl.CostEstimate(flops=55_000_000, bytes_accessed=2_000_000, transcendentals=0),
        name="expander",
    )(*arrays)


def plane(value):
    return lax.all_to_all(value, ("x", "y"), split_axis=0, concat_axis=0, tiled=True)


def per_device(
    inputs, gate_grad, up_grad, gate_codes, up_codes, gate_scale, up_scale,
    gate_down, gate_lift, up_down, up_lift,
):
    hid = lax.axis_index("hid")
    x, zh, y, core = (lax.axis_index(name) for name in FFN)
    place = jnp.stack([zh, core, hid, x, y])
    downs = gate_down.T, up_down.T

    both, back_other, back_own = prep(
        place, gate_grad.T, up_grad.T, gate_scale, up_scale, gate_lift, up_lift
    )
    two, one = swap(both, "hid", 2), swap(both, "hid", 1)
    gathered = spread(inputs, back_own, swap(back_other, "core", 1))

    landed = plane(gathered)
    both, two, one, landed, marked = lax.optimization_barrier(
        (both, two, one, landed, mark(one, two))
    )
    middle = lax.ppermute(both, "hid", [(1, 2), (2, 1)])
    ends = lax.ppermute(two, "hid", [(1, 0), (2, 3)])

    codes = gate_codes.T, up_codes.T
    small = narrow(marked, landed, *downs)
    small_theirs = swap(small, "zh", 1)
    other1, own1, grads1 = product((both, one, two), 1, *codes)
    other1, middle, ends, small_theirs, marked = lax.optimization_barrier(
        (other1, middle, ends, small_theirs, mark(middle, ends, small_theirs))
    )
    other2, own2, grads2 = product((middle, ends), 2, *codes)
    own2, small_theirs = lax.optimization_barrier((own2, small_theirs))
    sums = add_pairs(
        marked, place, own1, swap(other1, "core", 1), own2, swap(other2, "core", 1)
    )

    parts = gather_over(join_halves(small, small_theirs), "hid")
    marked, parts = lax.optimization_barrier((sums, parts))
    kept = plane(sums.reshape(256, FEATS)).astype(F32).reshape(16, 16, FEATS).sum(0)
    low, adapter, keep, give = joined(marked, place, parts, landed, *downs)
    low_other = swap(low, "core", 1)
    half = (keep + swap(give, "core", 1)).astype(BF16)
    mine = half.astype(F32) + swap(half, "zh", 1).astype(F32)
    theirs = swap(mine, "core", 1)
    gate_reducer, up_reducer = (jnp.where(core == k, mine, theirs) for k in range(2))
    gate_expander, up_expander = expander(
        place, low_other, low, grads1, grads2, gate_scale, up_scale
    )
    arrived = swap(kept[:8].astype(BF16), "zh", 1)
    rows = (kept[8:] + arrived.astype(F32) + adapter).astype(BF16)
    return rows, gate_reducer.T, gate_expander, up_reducer.T, up_expander


def solution(mesh):
    whole = Mesh(mesh.devices.reshape(4, 4, 2, 4, 2), ("hid",) + FFN)
    placed = (
        P(FFN, "hid"), P("hid", FFN), P("hid", FFN), P("hid", FFN), P("hid", FFN),
        P(FFN), P(FFN), P("hid", None), P(None, FFN), P("hid", None), P(None, FFN),
    )
    return jax.shard_map(
        per_device,
        mesh=whole,
        in_specs=placed,
        out_specs=(P(FFN, "hid"), P("hid", None), P(None, FFN), P("hid", None), P(None, FFN)),
        check_vma=False,
    )
```

```python
import functools

import jax
import jax.numpy as jnp
from jax import lax
from jax.experimental import pallas as pl
from jax.experimental.pallas import tpu as pltpu
from jax.sharding import Mesh, PartitionSpec as P

ADAPTER_SCALE = 2.0
FFN = ("x", "zh", "y", "core")
F32, BF16 = jnp.float32, jnp.bfloat16
UNITS, BOTH, FEATS, STEP, CHUNK = 832, 1664, 2048, 256, 512
PLAIN = (((1,), (0,)), ((), ()))
BY_ROWS = (((1,), (1,)), ((), ()))
BY_COLUMNS = (((0,), (0,)), ((), ()))
SMEM = pl.BlockSpec(memory_space=pltpu.SMEM)
VMEM = pl.BlockSpec(memory_space=pltpu.VMEM)


def swap(value, axis, mask):
    size = lax.axis_size(axis)
    return lax.ppermute(value, axis, [(i, i ^ mask) for i in range(size)])


def gather_over(value, axis):
    return [value] + [swap(value, axis, k) for k in range(1, lax.axis_size(axis))]


def dot(left, right, how):
    return lax.dot_general(left, right, how, preferred_element_type=F32)


def one_hot(rows, columns, source):
    row = lax.broadcasted_iota(jnp.int32, (rows, columns), 0)
    column = lax.broadcasted_iota(jnp.int32, (rows, columns), 1)
    return (column == source(row)).astype(F32).astype(BF16)


def prep_kernel(place, gate, up, gate_scale, up_scale, gate_lift, up_lift, both, back_sums):
    zh, core = place[0], place[1]

    def source(row):
        half, side = 1 - row // 64, 1 - row // 32 % 2
        return (half ^ zh) * 64 + row // 8 % 4 * 16 + (side ^ core) * 8 + row % 8

    order = one_hot(128, 128, source)
    none = jnp.zeros((16, UNITS), F32)
    lifts = (
        jnp.concatenate([gate_lift[...], none], 0).astype(BF16),
        jnp.concatenate([none, up_lift[...]], 0).astype(BF16),
    )
    back, scaled = jnp.zeros((128, 32), F32), []
    for k, (grad, scale) in enumerate(((gate, gate_scale), (up, up_scale))):
        rows = dot(order, grad[...], BY_ROWS)
        back += dot(rows.astype(BF16), lifts[k], BY_ROWS)
        scaled.append(rows * scale[...].reshape(1, UNITS))
    both[...] = jnp.concatenate(scaled, 1).astype(BF16).reshape(2, 2, 32, BOTH)

    def packed(row):
        return row // 4 % 2 * 64 + row // 8 % 2 * 32 + row % 4 * 8 + row // 16

    back = dot(one_hot(128, 128, packed), back.astype(BF16), PLAIN)
    for c in range(2):
        rows = [back[16 * i + 8 * (1 - c) : 16 * i + 8 * (2 - c)] for i in range(8)]
        back_sums[8 * c : 8 * c + 8] = jnp.concatenate(rows, 1)


def prep(place, *arrays):
    both = jax.ShapeDtypeStruct((2, 2, 32, BOTH), BF16)
    back = jax.ShapeDtypeStruct((16, 256), F32)
    return pl.pallas_call(
        prep_kernel,
        out_shape=(both, back),
        in_specs=[SMEM] + [VMEM] * 6,
        out_specs=(VMEM,) * 2,
        cost_estimate=pl.CostEstimate(flops=14_000_000, bytes_accessed=1_200_000, transcendentals=0),
        name="prep",
    )(place, *arrays)


def product_kernel(pairs, *refs):
    blocks, (gate_codes, up_codes, other, own, grads, held, sems) = refs[:-7], refs[-7:]
    count = len(blocks) // pairs

    def copies(i):
        columns = pl.ds(i * CHUNK, CHUNK)
        return [
            pltpu.make_async_copy(
                source.at[:, columns], held.at[pl.ds(k * UNITS, UNITS), columns], sems.at[k, i]
            )
            for k, source in enumerate((gate_codes, up_codes))
        ]

    for copy in copies(0) + copies(1):
        copy.start()
    for c in range(2):
        for half in range(2):
            for j in range(count):
                value = blocks[j * pairs][half, c]
                if pairs == 2:
                    value += blocks[j * pairs + 1][half, c]
                row = ((c * 2 + half) * count + j) * 32
                grads[row : row + 32] = value
    rows, cut = grads[...], 64 * count
    for start in range(0, FEATS, STEP):
        columns = slice(start, start + STEP)
        if start % CHUNK == 0:
            i = start // CHUNK
            for copy in copies(i):
                copy.wait()
            if i + 2 < FEATS // CHUNK:
                for copy in copies(i + 2):
                    copy.start()
        total = dot(rows, held[:, columns], PLAIN)
        other[:, columns] = total[:cut].astype(BF16)
        own[:, columns] = total[cut:].astype(BF16)


def product(blocks, pairs, gate_codes, up_codes):
    count = len(blocks) // pairs
    part = jax.ShapeDtypeStruct((64 * count, FEATS), BF16)
    anywhere = pl.BlockSpec(memory_space=pl.ANY)
    return pl.pallas_call(
        functools.partial(product_kernel, pairs),
        out_shape=(part, part, jax.ShapeDtypeStruct((128 * count, BOTH), BF16)),
        in_specs=[VMEM] * len(blocks) + [anywhere] * 2,
        out_specs=(VMEM,) * 3,
        scratch_shapes=[
            pltpu.VMEM((BOTH, FEATS), BF16),
            pltpu.SemaphoreType.DMA((2, FEATS // CHUNK)),
        ],
        compiler_params=pltpu.CompilerParams(vmem_limit_bytes=44 << 20),
        cost_estimate=pl.CostEstimate(
            flops=900_000_000 * count, bytes_accessed=8_000_000, transcendentals=0
        ),
        name="product",
    )(*blocks, gate_codes, up_codes)


def pairs_kernel(marked, place, own1, theirs1, own2, theirs2, out):
    for j in range(4):
        halves = []
        for half in range(2):
            own, theirs, row = (own1, theirs1, (half * 3 + j) * 32) if j < 3 else (own2, theirs2, half * 32)
            rows = slice(row, row + 32)
            halves.append(own[rows].astype(F32) + theirs[rows].astype(F32))
        for k in range(4):
            rows = slice(8 * k, 8 * k + 8)
            out[place[2] ^ j, k] = jnp.concatenate([half[rows] for half in halves], 0).astype(BF16)


def add_pairs(*arrays):
    return pl.pallas_call(
        pairs_kernel,
        out_shape=jax.ShapeDtypeStruct((4, 4, 16, FEATS), BF16),
        in_specs=[pl.BlockSpec(memory_space=pl.ANY), SMEM] + [VMEM] * 4,
        out_specs=VMEM,
        compiler_params=pltpu.CompilerParams(vmem_limit_bytes=8 << 20),
        cost_estimate=pl.CostEstimate(flops=600_000, bytes_accessed=3_200_000, transcendentals=0),
        name="add_pairs",
    )(*arrays)


def mark_kernel(*refs):
    refs[-1][...] = jnp.zeros((8, 128), F32)


def mark(*arrays):
    return pl.pallas_call(
        mark_kernel,
        out_shape=jax.ShapeDtypeStruct((8, 128), F32),
        in_specs=[pl.BlockSpec(memory_space=pl.ANY)] * len(arrays),
        out_specs=VMEM,
        compiler_params=pltpu.CompilerParams(vmem_limit_bytes=1 << 20),
        cost_estimate=pl.CostEstimate(flops=100_000_000_000, bytes_accessed=4096, transcendentals=0),
        name="mark",
    )(*arrays)


def spread_kernel(inputs, inputs_theirs, back, back_theirs, gate_down, up_down, out, down):
    tokens = jnp.concatenate([inputs[...].astype(F32), inputs_theirs[...].astype(F32)], 0)
    sums = back[...] + jnp.concatenate([back_theirs[8:], back_theirs[:8]], 0)
    rows = jnp.concatenate([tokens, sums], 1).astype(BF16)
    for i in range(16):
        out[16 * i : 16 * i + 16] = rows
    down[...] = jnp.concatenate([gate_down[...], up_down[...]], 0).astype(BF16)


def spread(*arrays):
    return pl.pallas_call(
        spread_kernel,
        out_shape=(
            jax.ShapeDtypeStruct((256, FEATS + 256), BF16),
            jax.ShapeDtypeStruct((32, FEATS), BF16),
        ),
        in_specs=[VMEM] * 6,
        out_specs=(VMEM, VMEM),
        compiler_params=pltpu.CompilerParams(vmem_limit_bytes=6 << 20),
        cost_estimate=pl.CostEstimate(flops=40_000_000_000, bytes_accessed=1_400_000, transcendentals=0),
        name="spread",
    )(*arrays)


def narrow_kernel(marked, landed, down, out):
    low = dot(down[...], landed[:, :FEATS], BY_ROWS)
    back = landed[:, FEATS:].astype(F32).reshape(16, 16, 256).sum(0)
    out[...] = jnp.concatenate([low, back], 0).astype(BF16)


def narrow(*arrays):
    return pl.pallas_call(
        narrow_kernel,
        out_shape=jax.ShapeDtypeStruct((48, 256), BF16),
        in_specs=[pl.BlockSpec(memory_space=pl.ANY)] + [VMEM] * 2,
        out_specs=VMEM,
        compiler_params=pltpu.CompilerParams(vmem_limit_bytes=6 << 20),
        cost_estimate=pl.CostEstimate(flops=17_000_000, bytes_accessed=900_000, transcendentals=0),
        name="narrow",
    )(*arrays)


def halves_kernel(own, theirs, out):
    mine, other = own[...].astype(F32), theirs[...].astype(F32)
    back = jnp.concatenate([other[start : start + 4] for start in (36, 32, 44, 40)], 0)
    out[...] = jnp.concatenate([mine[:32], other[:32], mine[32:] + back], 0).astype(BF16)


def join_halves(*arrays):
    return pl.pallas_call(
        halves_kernel,
        out_shape=jax.ShapeDtypeStruct((80, 256), BF16),
        in_specs=[VMEM] * 2,
        out_specs=VMEM,
        compiler_params=pltpu.CompilerParams(vmem_limit_bytes=2 << 20),
        cost_estimate=pl.CostEstimate(flops=10_000, bytes_accessed=80_000, transcendentals=0),
        name="join_halves",
    )(*arrays)


def joined_kernel(marked, place, p0, p1, p2, p3, landed, down, low_out, adapter, keep):
    core, hid, x, y = place[1], place[2], place[3], place[4]
    parts = [part[...].astype(F32) for part in (p0, p1, p2, p3)]
    low_out[...] = sum(part[:64] for part in parts).astype(BF16)
    back = jnp.concatenate(
        [part[64:80, 32 * i : 32 * i + 32] for part in parts for i in range(8)], 0
    ).astype(BF16)

    def source(row):
        return ((row // 64) ^ hid) * 128 + row % 8 * 16 + row // 8 % 2 * 8 + 4 + row // 16 % 4

    mine = dot(one_hot(16, 512, lambda row: source(x * 64 + y * 16 + row % 8)), back, PLAIN)
    back = (ADAPTER_SCALE * dot(one_hot(256, 512, source), back, PLAIN)).astype(BF16)
    adapter[...] = ADAPTER_SCALE * dot(mine.astype(BF16), down[...], PLAIN)[:8]
    reducer = dot(back, landed[:, :FEATS], BY_COLUMNS)
    keep[...] = jnp.where(core == 0, reducer[:16], reducer[16:]).astype(BF16)


def joined(marked, place, parts, *arrays):
    return pl.pallas_call(
        joined_kernel,
        out_shape=(
            jax.ShapeDtypeStruct((64, 256), BF16),
            jax.ShapeDtypeStruct((8, FEATS), F32),
            jax.ShapeDtypeStruct((16, FEATS), BF16),
        ),
        in_specs=[pl.BlockSpec(memory_space=pl.ANY), SMEM] + [VMEM] * 6,
        out_specs=(VMEM,) * 3,
        compiler_params=pltpu.CompilerParams(vmem_limit_bytes=8 << 20),
        cost_estimate=pl.CostEstimate(flops=40_000_000, bytes_accessed=1_400_000, transcendentals=0),
        name="joined",
    )(marked, place, *parts, *arrays)


def expander_kernel(place, low_halves, grads1, grads2, gate_scale, up_scale, gate_out, up_out):
    hid = place[2]
    low = jnp.concatenate([low_halves[:32], low_halves[32:]], 1)

    def order(blocks):
        pieces = [
            one_hot(
                32 * len(blocks),
                512,
                lambda row: (1 - half) * 256 + ((row // 32 + blocks[0]) ^ hid) * 64 + row // 8 % 4 * 16 + (1 - c) * 8 + row % 8,
            )
            for c in range(2)
            for half in range(2)
        ]
        return jnp.concatenate(pieces, 0)

    low1 = dot(low, order((0, 1, 2)), BY_ROWS).astype(BF16)
    low2 = dot(low, order((3,)), BY_ROWS).astype(BF16)
    total = ADAPTER_SCALE * (dot(low1, grads1[...], PLAIN) + dot(low2, grads2[...], PLAIN))
    gate_out[...] = total[:16, :UNITS] / gate_scale[...].reshape(1, UNITS)
    up_out[...] = total[16:, UNITS:] / up_scale[...].reshape(1, UNITS)


def expander(*arrays):
    out = jax.ShapeDtypeStruct((16, UNITS), F32)
    return pl.pallas_call(
        expander_kernel,
        out_shape=(out, out),
        in_specs=[SMEM] + [VMEM] * 5,
        out_specs=(VMEM, VMEM),
        compiler_params=pltpu.CompilerParams(vmem_limit_bytes=8 << 20),
        cost_estimate=pl.CostEstimate(flops=55_000_000, bytes_accessed=2_000_000, transcendentals=0),
        name="expander",
    )(*arrays)


def plane(value):
    return lax.all_to_all(value, ("x", "y"), split_axis=0, concat_axis=0, tiled=True)


def per_device(
    inputs, gate_grad, up_grad, gate_codes, up_codes, gate_scale, up_scale,
    gate_down, gate_lift, up_down, up_lift,
):
    hid = lax.axis_index("hid")
    x, zh, y, core = (lax.axis_index(name) for name in FFN)
    place = jnp.stack([zh, core, hid, x, y])

    inputs_theirs = swap(inputs, "core", 1)
    both, back = prep(place, gate_grad.T, up_grad.T, gate_scale, up_scale, gate_lift, up_lift)
    two, one = swap(both, "hid", 2), swap(both, "hid", 1)
    gathered, down = spread(
        inputs, inputs_theirs, back, swap(back, "core", 1), gate_down.T, up_down.T
    )

    landed = plane(gathered)
    both, two, one, marked = lax.optimization_barrier((both, two, one, mark(one, two)))
    middle = lax.ppermute(both, "hid", [(1, 2), (2, 1)])
    ends = lax.ppermute(two, "hid", [(1, 0), (2, 3)])

    codes = gate_codes.T, up_codes.T
    one, landed = lax.optimization_barrier((one, landed))
    small = narrow(marked, landed, down)
    small_theirs = swap(small, "zh", 1)
    other1, own1, grads1 = product((both, one, two), 1, *codes)
    other1, middle, ends, small_theirs, marked = lax.optimization_barrier(
        (other1, middle, ends, small_theirs, mark(middle, ends, small_theirs))
    )
    other2, own2, grads2 = product((middle, ends), 2, *codes)
    own2, small_theirs = lax.optimization_barrier((own2, small_theirs))
    sums = add_pairs(
        marked, place, own1, swap(other1, "core", 1), own2, swap(other2, "core", 1)
    )
    parts = gather_over(join_halves(small, small_theirs), "hid")
    marked, parts = lax.optimization_barrier((sums, parts))
    kept = plane(sums.reshape(256, FEATS)).astype(F32).reshape(16, 16, FEATS).sum(0)
    low, adapter, half = joined(marked, place, parts, landed, down)
    mine = half.astype(F32) + swap(half, "zh", 1).astype(F32)
    theirs = swap(mine, "core", 1)
    gate_reducer, up_reducer = (jnp.where(core == k, mine, theirs) for k in range(2))
    gate_expander, up_expander = expander(place, low, grads1, grads2, gate_scale, up_scale)
    arrived = swap(kept[:8].astype(BF16), "zh", 1)
    rows = (kept[8:] + arrived.astype(F32) + adapter).astype(BF16)
    return rows, gate_reducer.T, gate_expander, up_reducer.T, up_expander


def solution(mesh):
    whole = Mesh(mesh.devices.reshape(4, 4, 2, 4, 2), ("hid",) + FFN)
    placed = (
        P(FFN, "hid"), P("hid", FFN), P("hid", FFN), P("hid", FFN), P("hid", FFN),
        P(FFN), P(FFN), P("hid", None), P(None, FFN), P("hid", None), P(None, FFN),
    )
    return jax.shard_map(
        per_device,
        mesh=whole,
        in_specs=placed,
        out_specs=(P(FFN, "hid"), P("hid", None), P(None, FFN), P("hid", None), P(None, FFN)),
        check_vma=False,
    )
```

```python
import functools

import jax
import jax.numpy as jnp
from jax import lax
from jax.experimental import pallas as pl
from jax.experimental.pallas import tpu as pltpu
from jax.sharding import Mesh, PartitionSpec as P

ADAPTER_SCALE = 2.0
FFN = ("x", "zh", "y", "core")
F32, BF16 = jnp.float32, jnp.bfloat16
UNITS, BOTH, FEATS, STEP, CHUNK = 832, 1664, 2048, 256, 512
PLAIN = (((1,), (0,)), ((), ()))
BY_ROWS = (((1,), (1,)), ((), ()))
BY_COLUMNS = (((0,), (0,)), ((), ()))
SMEM = pl.BlockSpec(memory_space=pltpu.SMEM)
VMEM = pl.BlockSpec(memory_space=pltpu.VMEM)


def swap(value, axis, mask):
    size = lax.axis_size(axis)
    return lax.ppermute(value, axis, [(i, i ^ mask) for i in range(size)])


def gather_over(value, axis):
    return [value] + [swap(value, axis, k) for k in range(1, lax.axis_size(axis))]


def dot(left, right, how):
    return lax.dot_general(left, right, how, preferred_element_type=F32)


def one_hot(rows, columns, source):
    row = lax.broadcasted_iota(jnp.int32, (rows, columns), 0)
    column = lax.broadcasted_iota(jnp.int32, (rows, columns), 1)
    return (column == source(row)).astype(F32).astype(BF16)


def prep_kernel(place, gate, up, gate_scale, up_scale, gate_lift, up_lift, both, back_sums):
    zh, core = place[0], place[1]

    def source(row):
        half, side = 1 - row // 64, 1 - row // 32 % 2
        return (half ^ zh) * 64 + row // 8 % 4 * 16 + (side ^ core) * 8 + row % 8

    order = one_hot(128, 128, source)
    none = jnp.zeros((16, UNITS), F32)
    lifts = (
        jnp.concatenate([gate_lift[...], none], 0).astype(BF16),
        jnp.concatenate([none, up_lift[...]], 0).astype(BF16),
    )
    back, scaled = jnp.zeros((128, 32), F32), []
    for k, (grad, scale) in enumerate(((gate, gate_scale), (up, up_scale))):
        rows = dot(order, grad[...], BY_ROWS)
        back += dot(rows.astype(BF16), lifts[k], BY_ROWS)
        scaled.append(rows * scale[...].reshape(1, UNITS))
    both[...] = jnp.concatenate(scaled, 1).astype(BF16).reshape(2, 2, 32, BOTH)

    def packed(row):
        return row // 4 % 2 * 64 + row // 8 % 2 * 32 + row % 4 * 8 + row // 16

    back = dot(one_hot(128, 128, packed), back.astype(BF16), PLAIN)
    for c in range(2):
        rows = [back[16 * i + 8 * (1 - c) : 16 * i + 8 * (2 - c)] for i in range(8)]
        back_sums[8 * c : 8 * c + 8] = jnp.concatenate(rows, 1)


def prep(place, *arrays):
    both = jax.ShapeDtypeStruct((2, 2, 32, BOTH), BF16)
    back = jax.ShapeDtypeStruct((16, 256), F32)
    return pl.pallas_call(
        prep_kernel,
        out_shape=(both, back),
        in_specs=[SMEM] + [VMEM] * 6,
        out_specs=(VMEM,) * 2,
        cost_estimate=pl.CostEstimate(flops=14_000_000, bytes_accessed=1_200_000, transcendentals=0),
        name="prep",
    )(place, *arrays)


def product_kernel(pairs, *refs):
    blocks, (gate_codes, up_codes, other, own, grads, held, sems) = refs[:-7], refs[-7:]
    count = len(blocks) // pairs

    def copies(i):
        columns = pl.ds(i * CHUNK, CHUNK)
        return [
            pltpu.make_async_copy(
                source.at[:, columns], held.at[pl.ds(k * UNITS, UNITS), columns], sems.at[k, i]
            )
            for k, source in enumerate((gate_codes, up_codes))
        ]

    for copy in copies(0) + copies(1):
        copy.start()
    for c in range(2):
        for half in range(2):
            for j in range(count):
                value = blocks[j * pairs][half, c]
                if pairs == 2:
                    value += blocks[j * pairs + 1][half, c]
                row = ((c * 2 + half) * count + j) * 32
                grads[row : row + 32] = value
    rows, cut = grads[...], 64 * count
    for start in range(0, FEATS, STEP):
        columns = slice(start, start + STEP)
        if start % CHUNK == 0:
            i = start // CHUNK
            for copy in copies(i):
                copy.wait()
            if i + 2 < FEATS // CHUNK:
                for copy in copies(i + 2):
                    copy.start()
        total = dot(rows, held[:, columns], PLAIN)
        other[:, columns] = total[:cut].astype(BF16)
        own[:, columns] = total[cut:].astype(BF16)


def product(blocks, pairs, gate_codes, up_codes):
    count = len(blocks) // pairs
    part = jax.ShapeDtypeStruct((64 * count, FEATS), BF16)
    anywhere = pl.BlockSpec(memory_space=pl.ANY)
    return pl.pallas_call(
        functools.partial(product_kernel, pairs),
        out_shape=(part, part, jax.ShapeDtypeStruct((128 * count, BOTH), BF16)),
        in_specs=[VMEM] * len(blocks) + [anywhere] * 2,
        out_specs=(VMEM,) * 3,
        scratch_shapes=[
            pltpu.VMEM((BOTH, FEATS), BF16),
            pltpu.SemaphoreType.DMA((2, FEATS // CHUNK)),
        ],
        compiler_params=pltpu.CompilerParams(vmem_limit_bytes=44 << 20),
        cost_estimate=pl.CostEstimate(
            flops=900_000_000 * count, bytes_accessed=8_000_000, transcendentals=0
        ),
        name="product",
    )(*blocks, gate_codes, up_codes)


def pairs_kernel(marked, place, own1, theirs1, own2, theirs2, out):
    for j in range(4):
        halves = []
        for half in range(2):
            own, theirs, row = (own1, theirs1, (half * 3 + j) * 32) if j < 3 else (own2, theirs2, half * 32)
            rows = slice(row, row + 32)
            halves.append(own[rows].astype(F32) + theirs[rows].astype(F32))
        for k in range(4):
            rows = slice(8 * k, 8 * k + 8)
            out[place[2] ^ j, k] = jnp.concatenate([half[rows] for half in halves], 0).astype(BF16)


def add_pairs(*arrays):
    return pl.pallas_call(
        pairs_kernel,
        out_shape=jax.ShapeDtypeStruct((4, 4, 16, FEATS), BF16),
        in_specs=[pl.BlockSpec(memory_space=pl.ANY), SMEM] + [VMEM] * 4,
        out_specs=VMEM,
        compiler_params=pltpu.CompilerParams(vmem_limit_bytes=8 << 20),
        cost_estimate=pl.CostEstimate(flops=600_000, bytes_accessed=3_200_000, transcendentals=0),
        name="add_pairs",
    )(*arrays)


def mark_kernel(*refs):
    refs[-1][...] = jnp.zeros((8, 128), F32)


def mark(*arrays):
    return pl.pallas_call(
        mark_kernel,
        out_shape=jax.ShapeDtypeStruct((8, 128), F32),
        in_specs=[pl.BlockSpec(memory_space=pl.ANY)] * len(arrays),
        out_specs=VMEM,
        compiler_params=pltpu.CompilerParams(vmem_limit_bytes=1 << 20),
        cost_estimate=pl.CostEstimate(flops=100_000_000_000, bytes_accessed=4096, transcendentals=0),
        name="mark",
    )(*arrays)


def spread_kernel(inputs, inputs_theirs, back, back_theirs, gate_down, up_down, out, down):
    tokens = jnp.concatenate([inputs[...].astype(F32), inputs_theirs[...].astype(F32)], 0)
    sums = back[...] + jnp.concatenate([back_theirs[8:], back_theirs[:8]], 0)
    rows = jnp.concatenate([tokens, sums], 1).astype(BF16)
    for i in range(16):
        out[16 * i : 16 * i + 16] = rows
    down[...] = jnp.concatenate([gate_down[...], up_down[...]], 0).astype(BF16)


def spread(*arrays):
    return pl.pallas_call(
        spread_kernel,
        out_shape=(
            jax.ShapeDtypeStruct((256, FEATS + 256), BF16),
            jax.ShapeDtypeStruct((32, FEATS), BF16),
        ),
        in_specs=[VMEM] * 6,
        out_specs=(VMEM, VMEM),
        compiler_params=pltpu.CompilerParams(vmem_limit_bytes=6 << 20),
        cost_estimate=pl.CostEstimate(flops=40_000_000_000, bytes_accessed=1_400_000, transcendentals=0),
        name="spread",
    )(*arrays)


def narrow_kernel(marked, landed, down, out):
    low = dot(down[...], landed[:, :FEATS], BY_ROWS)
    back = landed[:, FEATS:].astype(F32).reshape(16, 16, 256).sum(0)
    out[...] = jnp.concatenate([low, back], 0).astype(BF16)


def narrow(*arrays):
    return pl.pallas_call(
        narrow_kernel,
        out_shape=jax.ShapeDtypeStruct((48, 256), BF16),
        in_specs=[pl.BlockSpec(memory_space=pl.ANY)] + [VMEM] * 2,
        out_specs=VMEM,
        compiler_params=pltpu.CompilerParams(vmem_limit_bytes=6 << 20),
        cost_estimate=pl.CostEstimate(flops=17_000_000, bytes_accessed=900_000, transcendentals=0),
        name="narrow",
    )(*arrays)


def halves_kernel(own, theirs, out):
    mine, other = own[...].astype(F32), theirs[...].astype(F32)
    back = jnp.concatenate([other[start : start + 4] for start in (36, 32, 44, 40)], 0)
    out[...] = jnp.concatenate([mine[:32], other[:32], mine[32:] + back], 0).astype(BF16)


def join_halves(*arrays):
    return pl.pallas_call(
        halves_kernel,
        out_shape=jax.ShapeDtypeStruct((80, 256), BF16),
        in_specs=[VMEM] * 2,
        out_specs=VMEM,
        compiler_params=pltpu.CompilerParams(vmem_limit_bytes=2 << 20),
        cost_estimate=pl.CostEstimate(flops=10_000, bytes_accessed=80_000, transcendentals=0),
        name="join_halves",
    )(*arrays)


def joined_kernel(marked, place, p0, p1, p2, p3, landed, down, low_out, adapter, keep):
    core, hid, x, y = place[1], place[2], place[3], place[4]
    parts = [part[...].astype(F32) for part in (p0, p1, p2, p3)]
    low_out[...] = sum(part[:64] for part in parts).astype(BF16)
    back = jnp.concatenate(
        [part[64:80, 32 * i : 32 * i + 32] for part in parts for i in range(8)], 0
    ).astype(BF16)

    def source(row):
        return ((row // 64) ^ hid) * 128 + row % 8 * 16 + row // 8 % 2 * 8 + 4 + row // 16 % 4

    mine = dot(one_hot(16, 512, lambda row: source(x * 64 + y * 16 + row % 8)), back, PLAIN)
    back = (ADAPTER_SCALE * dot(one_hot(256, 512, source), back, PLAIN)).astype(BF16)
    adapter[...] = ADAPTER_SCALE * dot(mine.astype(BF16), down[...], PLAIN)[:8]
    reducer = dot(back, landed[:, :FEATS], BY_COLUMNS)
    keep[...] = jnp.where(core == 0, reducer[:16], reducer[16:]).astype(BF16)


def joined(marked, place, parts, *arrays):
    return pl.pallas_call(
        joined_kernel,
        out_shape=(
            jax.ShapeDtypeStruct((64, 256), BF16),
            jax.ShapeDtypeStruct((8, FEATS), F32),
            jax.ShapeDtypeStruct((16, FEATS), BF16),
        ),
        in_specs=[pl.BlockSpec(memory_space=pl.ANY), SMEM] + [VMEM] * 6,
        out_specs=(VMEM,) * 3,
        compiler_params=pltpu.CompilerParams(vmem_limit_bytes=8 << 20),
        cost_estimate=pl.CostEstimate(flops=40_000_000, bytes_accessed=1_400_000, transcendentals=0),
        name="joined",
    )(marked, place, *parts, *arrays)


def expander_kernel(place, low_halves, grads1, grads2, gate_scale, up_scale, gate_out, up_out):
    hid = place[2]
    low = jnp.concatenate([low_halves[:32], low_halves[32:]], 1)

    def order(blocks):
        pieces = [
            one_hot(
                32 * len(blocks),
                512,
                lambda row: (1 - half) * 256 + ((row // 32 + blocks[0]) ^ hid) * 64 + row // 8 % 4 * 16 + (1 - c) * 8 + row % 8,
            )
            for c in range(2)
            for half in range(2)
        ]
        return jnp.concatenate(pieces, 0)

    low1 = dot(low, order((0, 1, 2)), BY_ROWS).astype(BF16)
    low2 = dot(low, order((3,)), BY_ROWS).astype(BF16)
    total = ADAPTER_SCALE * (dot(low1, grads1[...], PLAIN) + dot(low2, grads2[...], PLAIN))
    gate_out[...] = total[:16, :UNITS] / gate_scale[...].reshape(1, UNITS)
    up_out[...] = total[16:, UNITS:] / up_scale[...].reshape(1, UNITS)


def expander(*arrays):
    out = jax.ShapeDtypeStruct((16, UNITS), F32)
    return pl.pallas_call(
        expander_kernel,
        out_shape=(out, out),
        in_specs=[SMEM] + [VMEM] * 5,
        out_specs=(VMEM, VMEM),
        compiler_params=pltpu.CompilerParams(vmem_limit_bytes=8 << 20),
        cost_estimate=pl.CostEstimate(flops=55_000_000, bytes_accessed=2_000_000, transcendentals=0),
        name="expander",
    )(*arrays)


def plane(value):
    return lax.all_to_all(value, ("x", "y"), split_axis=0, concat_axis=0, tiled=True)


def per_device(
    inputs, gate_grad, up_grad, gate_codes, up_codes, gate_scale, up_scale,
    gate_down, gate_lift, up_down, up_lift,
):
    hid = lax.axis_index("hid")
    x, zh, y, core = (lax.axis_index(name) for name in FFN)
    place = jnp.stack([zh, core, hid, x, y])

    inputs_theirs = swap(inputs, "core", 1)
    both, back = prep(place, gate_grad.T, up_grad.T, gate_scale, up_scale, gate_lift, up_lift)
    two, one = swap(both, "hid", 2), swap(both, "hid", 1)
    gathered, down = spread(
        inputs, inputs_theirs, back, swap(back, "core", 1), gate_down.T, up_down.T
    )

    landed = plane(gathered)
    both, two, one, marked = lax.optimization_barrier((both, two, one, mark(one, two)))
    middle = lax.ppermute(both, "hid", [(1, 2), (2, 1)])
    ends = lax.ppermute(two, "hid", [(1, 0), (2, 3)])

    codes = gate_codes.T, up_codes.T
    other1, own1, grads1 = product((both, one, two), 1, *codes)
    landed, grads1 = lax.optimization_barrier((landed, grads1))
    small = narrow(marked, landed, down)
    small_theirs = swap(small, "zh", 1)
    middle, ends, small_theirs, marked = lax.optimization_barrier(
        (middle, ends, small_theirs, mark(middle, ends, small_theirs))
    )
    other2, own2, grads2 = product((middle, ends), 2, *codes)
    own2, small_theirs = lax.optimization_barrier((own2, small_theirs))
    sums = add_pairs(
        marked, place, own1, swap(other1, "core", 1), own2, swap(other2, "core", 1)
    )
    parts = gather_over(join_halves(small, small_theirs), "hid")
    marked, parts = lax.optimization_barrier((sums, parts))
    kept = plane(sums.reshape(256, FEATS)).astype(F32).reshape(16, 16, FEATS).sum(0)
    low, adapter, half = joined(marked, place, parts, landed, down)
    half_theirs = swap(half, "zh", 1)
    half_theirs, kept = lax.optimization_barrier((half_theirs, kept))
    mine = half.astype(F32) + half_theirs.astype(F32)
    theirs = swap(mine, "core", 1)
    gate_reducer, up_reducer = (jnp.where(core == k, mine, theirs) for k in range(2))
    gate_expander, up_expander = expander(place, low, grads1, grads2, gate_scale, up_scale)
    arrived = swap(kept[:8].astype(BF16), "zh", 1)
    rows = (kept[8:] + arrived.astype(F32) + adapter).astype(BF16)
    return rows, gate_reducer.T, gate_expander, up_reducer.T, up_expander


def solution(mesh):
    whole = Mesh(mesh.devices.reshape(4, 4, 2, 4, 2), ("hid",) + FFN)
    placed = (
        P(FFN, "hid"), P("hid", FFN), P("hid", FFN), P("hid", FFN), P("hid", FFN),
        P(FFN), P(FFN), P("hid", None), P(None, FFN), P("hid", None), P(None, FFN),
    )
    return jax.shard_map(
        per_device,
        mesh=whole,
        in_specs=placed,
        out_specs=(P(FFN, "hid"), P("hid", None), P(None, FFN), P("hid", None), P(None, FFN)),
        check_vma=False,
    )
```

```python
import functools

import jax
import jax.numpy as jnp
from jax import lax
from jax.experimental import pallas as pl
from jax.experimental.pallas import tpu as pltpu
from jax.sharding import Mesh, PartitionSpec as P

ADAPTER_SCALE = 2.0
FFN = ("x", "zh", "y", "core")
F32, BF16 = jnp.float32, jnp.bfloat16
UNITS, BOTH, FEATS, STEP, CHUNK = 832, 1664, 2048, 256, 512
PLAIN = (((1,), (0,)), ((), ()))
BY_ROWS = (((1,), (1,)), ((), ()))
BY_COLUMNS = (((0,), (0,)), ((), ()))
SMEM = pl.BlockSpec(memory_space=pltpu.SMEM)
VMEM = pl.BlockSpec(memory_space=pltpu.VMEM)


def swap(value, axis, mask):
    size = lax.axis_size(axis)
    return lax.ppermute(value, axis, [(i, i ^ mask) for i in range(size)])


def gather_over(value, axis):
    return [value] + [swap(value, axis, k) for k in range(1, lax.axis_size(axis))]


def dot(left, right, how):
    return lax.dot_general(left, right, how, preferred_element_type=F32)


def one_hot(rows, columns, source):
    row = lax.broadcasted_iota(jnp.int32, (rows, columns), 0)
    column = lax.broadcasted_iota(jnp.int32, (rows, columns), 1)
    return (column == source(row)).astype(F32).astype(BF16)


def prep_kernel(place, gate, up, gate_scale, up_scale, gate_lift, up_lift, both, back_other, back_own):
    zh, core = place[0], place[1]

    def source(row):
        half, side = 1 - row // 64, 1 - row // 32 % 2
        return (half ^ zh) * 64 + row // 8 % 4 * 16 + (side ^ core) * 8 + row % 8

    order = one_hot(128, 128, source)
    none = jnp.zeros((16, UNITS), F32)
    lifts = (
        jnp.concatenate([gate_lift[...], none], 0).astype(BF16),
        jnp.concatenate([none, up_lift[...]], 0).astype(BF16),
    )
    back, scaled = jnp.zeros((128, 32), F32), []
    for k, (grad, scale) in enumerate(((gate, gate_scale), (up, up_scale))):
        rows = dot(order, grad[...], BY_ROWS)
        back += dot(rows.astype(BF16), lifts[k], BY_ROWS)
        scaled.append(rows * scale[...].reshape(1, UNITS))
    both[...] = jnp.concatenate(scaled, 1).astype(BF16).reshape(2, 2, 32, BOTH)

    def packed(row):
        return row // 4 % 2 * 64 + row // 8 % 2 * 32 + row % 4 * 8 + row // 16

    back = dot(one_hot(128, 128, packed), back.astype(BF16), PLAIN)
    back_other[...] = jnp.concatenate([back[16 * i : 16 * i + 8] for i in range(8)], 1)
    back_own[...] = jnp.concatenate([back[16 * i + 8 : 16 * i + 16] for i in range(8)], 1)


def prep(place, *arrays):
    both = jax.ShapeDtypeStruct((2, 2, 32, BOTH), BF16)
    back = jax.ShapeDtypeStruct((8, 256), F32)
    return pl.pallas_call(
        prep_kernel,
        out_shape=(both, back, back),
        in_specs=[SMEM] + [VMEM] * 6,
        out_specs=(VMEM,) * 3,
        cost_estimate=pl.CostEstimate(flops=14_000_000, bytes_accessed=1_200_000, transcendentals=0),
        name="prep",
    )(place, *arrays)


def product_kernel(pairs, *refs):
    blocks, (gate_codes, up_codes, other, own, grads, held, sems) = refs[:-7], refs[-7:]
    count = len(blocks) // pairs

    def copies(i):
        columns = pl.ds(i * CHUNK, CHUNK)
        return [
            pltpu.make_async_copy(
                source.at[:, columns], held.at[pl.ds(k * UNITS, UNITS), columns], sems.at[k, i]
            )
            for k, source in enumerate((gate_codes, up_codes))
        ]

    for copy in copies(0) + copies(1):
        copy.start()
    for c in range(2):
        for half in range(2):
            for j in range(count):
                value = blocks[j * pairs][half, c]
                if pairs == 2:
                    value += blocks[j * pairs + 1][half, c]
                row = ((c * 2 + half) * count + j) * 32
                grads[row : row + 32] = value
    rows, cut = grads[...], 64 * count
    for start in range(0, FEATS, STEP):
        columns = slice(start, start + STEP)
        if start % CHUNK == 0:
            i = start // CHUNK
            for copy in copies(i):
                copy.wait()
            if i + 2 < FEATS // CHUNK:
                for copy in copies(i + 2):
                    copy.start()
        total = dot(rows, held[:, columns], PLAIN)
        other[:, columns] = total[:cut].astype(BF16)
        own[:, columns] = total[cut:].astype(BF16)


def product(blocks, pairs, gate_codes, up_codes):
    count = len(blocks) // pairs
    part = jax.ShapeDtypeStruct((64 * count, FEATS), BF16)
    anywhere = pl.BlockSpec(memory_space=pl.ANY)
    return pl.pallas_call(
        functools.partial(product_kernel, pairs),
        out_shape=(part, part, jax.ShapeDtypeStruct((128 * count, BOTH), BF16)),
        in_specs=[VMEM] * len(blocks) + [anywhere] * 2,
        out_specs=(VMEM,) * 3,
        scratch_shapes=[
            pltpu.VMEM((BOTH, FEATS), BF16),
            pltpu.SemaphoreType.DMA((2, FEATS // CHUNK)),
        ],
        compiler_params=pltpu.CompilerParams(vmem_limit_bytes=44 << 20),
        cost_estimate=pl.CostEstimate(
            flops=900_000_000 * count, bytes_accessed=8_000_000, transcendentals=0
        ),
        name="product",
    )(*blocks, gate_codes, up_codes)


def pairs_kernel(marked, place, own1, theirs1, own2, theirs2, out):
    for j in range(4):
        halves = []
        for half in range(2):
            own, theirs, row = (own1, theirs1, (half * 3 + j) * 32) if j < 3 else (own2, theirs2, half * 32)
            rows = slice(row, row + 32)
            halves.append(own[rows].astype(F32) + theirs[rows].astype(F32))
        for k in range(4):
            rows = slice(8 * k, 8 * k + 8)
            out[place[2] ^ j, k] = jnp.concatenate([half[rows] for half in halves], 0).astype(BF16)


def add_pairs(*arrays):
    return pl.pallas_call(
        pairs_kernel,
        out_shape=jax.ShapeDtypeStruct((4, 4, 16, FEATS), BF16),
        in_specs=[pl.BlockSpec(memory_space=pl.ANY), SMEM] + [VMEM] * 4,
        out_specs=VMEM,
        compiler_params=pltpu.CompilerParams(vmem_limit_bytes=8 << 20),
        cost_estimate=pl.CostEstimate(flops=600_000, bytes_accessed=3_200_000, transcendentals=0),
        name="add_pairs",
    )(*arrays)


def mark_kernel(*refs):
    refs[-1][...] = jnp.zeros((8, 128), F32)


def mark(*arrays):
    return pl.pallas_call(
        mark_kernel,
        out_shape=jax.ShapeDtypeStruct((8, 128), F32),
        in_specs=[pl.BlockSpec(memory_space=pl.ANY)] * len(arrays),
        out_specs=VMEM,
        compiler_params=pltpu.CompilerParams(vmem_limit_bytes=1 << 20),
        cost_estimate=pl.CostEstimate(flops=100_000_000_000, bytes_accessed=4096, transcendentals=0),
        name="mark",
    )(*arrays)


def spread_kernel(inputs, back_own, back_theirs, gate_down, up_down, out, down):
    rows = jnp.concatenate([inputs[...].astype(F32), back_own[...] + back_theirs[...]], 1)
    rows = jnp.concatenate([rows, rows], 0).astype(BF16)
    for i in range(8):
        out[16 * i : 16 * i + 16] = rows
    down[...] = jnp.concatenate([gate_down[...], up_down[...]], 0).astype(BF16)


def spread(*arrays):
    return pl.pallas_call(
        spread_kernel,
        out_shape=(
            jax.ShapeDtypeStruct((128, FEATS + 256), BF16),
            jax.ShapeDtypeStruct((32, FEATS), BF16),
        ),
        in_specs=[VMEM] * 5,
        out_specs=(VMEM, VMEM),
        compiler_params=pltpu.CompilerParams(vmem_limit_bytes=4 << 20),
        cost_estimate=pl.CostEstimate(flops=40_000_000_000, bytes_accessed=700_000, transcendentals=0),
        name="spread",
    )(*arrays)


def narrow_kernel(marked, landed, down, out):
    low = dot(down[...], landed[:, :FEATS], BY_ROWS)
    back = landed[:, FEATS:].astype(F32).reshape(16, 8, 256).sum(0)
    low = jnp.concatenate([low, jnp.zeros((32, 128), F32)], 1)
    out[...] = jnp.concatenate([low, back, jnp.zeros((8, 256), F32)], 0).astype(BF16)


def narrow(*arrays):
    return pl.pallas_call(
        narrow_kernel,
        out_shape=jax.ShapeDtypeStruct((48, 256), BF16),
        in_specs=[pl.BlockSpec(memory_space=pl.ANY)] + [VMEM] * 2,
        out_specs=VMEM,
        compiler_params=pltpu.CompilerParams(vmem_limit_bytes=6 << 20),
        cost_estimate=pl.CostEstimate(flops=17_000_000, bytes_accessed=900_000, transcendentals=0),
        name="narrow",
    )(*arrays)


def halves_kernel(own, theirs, out):
    mine, other = own[...].astype(F32), theirs[...].astype(F32)
    low = jnp.concatenate([mine[:32, :128], other[:32, :128]], 1)
    back = mine[32:40] + jnp.concatenate([other[36:40], other[32:36]], 0)
    out[...] = jnp.concatenate([low, back, jnp.zeros((8, 256), F32)], 0).astype(BF16)


def join_halves(*arrays):
    return pl.pallas_call(
        halves_kernel,
        out_shape=jax.ShapeDtypeStruct((48, 256), BF16),
        in_specs=[VMEM] * 2,
        out_specs=VMEM,
        compiler_params=pltpu.CompilerParams(vmem_limit_bytes=2 << 20),
        cost_estimate=pl.CostEstimate(flops=10_000, bytes_accessed=80_000, transcendentals=0),
        name="join_halves",
    )(*arrays)


def joined_kernel(marked, place, p0, p1, p2, p3, landed, down, low_out, adapter, keep, give):
    core, hid, x, y = place[1], place[2], place[3], place[4]
    parts = [part[...].astype(F32) for part in (p0, p1, p2, p3)]
    low_out[...] = sum(part[:32] for part in parts).astype(BF16)
    back = jnp.concatenate(
        [part[32:40, 32 * i : 32 * i + 32] for part in parts for i in range(8)], 0
    ).astype(BF16)

    def source(row):
        return ((row // 32) ^ hid) * 64 + row % 8 * 8 + 4 + row // 8 % 4

    mine = dot(one_hot(16, 256, lambda row: source(x * 32 + y * 8 + row % 8)), back, PLAIN)
    back = (ADAPTER_SCALE * dot(one_hot(128, 256, source), back, PLAIN)).astype(BF16)
    adapter[...] = ADAPTER_SCALE * dot(mine.astype(BF16), down[...], PLAIN)[:8]
    reducer = dot(back, landed[:, :FEATS], BY_COLUMNS)
    keep[...] = jnp.where(core == 0, reducer[:16], reducer[16:])
    give[...] = jnp.where(core == 0, reducer[16:], reducer[:16])


def joined(marked, place, parts, *arrays):
    half = jax.ShapeDtypeStruct((16, FEATS), F32)
    return pl.pallas_call(
        joined_kernel,
        out_shape=(
            jax.ShapeDtypeStruct((32, 256), BF16),
            jax.ShapeDtypeStruct((8, FEATS), F32),
            half,
            half,
        ),
        in_specs=[pl.BlockSpec(memory_space=pl.ANY), SMEM] + [VMEM] * 6,
        out_specs=(VMEM,) * 4,
        compiler_params=pltpu.CompilerParams(vmem_limit_bytes=6 << 20),
        cost_estimate=pl.CostEstimate(flops=100_000_000_000, bytes_accessed=1_000_000, transcendentals=0),
        name="joined",
    )(marked, place, *parts, *arrays)


def expander_kernel(place, low_other, low_own, grads1, grads2, gate_scale, up_scale, gate_out, up_out):
    hid = place[2]
    low = jnp.concatenate([low_other[...], low_own[...]], 1)

    def order(blocks):
        pieces = [
            one_hot(
                32 * len(blocks),
                512,
                lambda row: c * 256 + (1 - half) * 128 + ((row // 32 + blocks[0]) ^ hid) * 32 + row % 32,
            )
            for c in range(2)
            for half in range(2)
        ]
        return jnp.concatenate(pieces, 0)

    low1 = dot(low, order((0, 1, 2)), BY_ROWS).astype(BF16)
    low2 = dot(low, order((3,)), BY_ROWS).astype(BF16)
    total = ADAPTER_SCALE * (dot(low1, grads1[...], PLAIN) + dot(low2, grads2[...], PLAIN))
    gate_out[...] = total[:16, :UNITS] / gate_scale[...].reshape(1, UNITS)
    up_out[...] = total[16:, UNITS:] / up_scale[...].reshape(1, UNITS)


def expander(*arrays):
    out = jax.ShapeDtypeStruct((16, UNITS), F32)
    return pl.pallas_call(
        expander_kernel,
        out_shape=(out, out),
        in_specs=[SMEM] + [VMEM] * 6,
        out_specs=(VMEM, VMEM),
        compiler_params=pltpu.CompilerParams(vmem_limit_bytes=8 << 20),
        cost_estimate=pl.CostEstimate(flops=55_000_000, bytes_accessed=2_000_000, transcendentals=0),
        name="expander",
    )(*arrays)


def plane(value):
    return lax.all_to_all(value, ("x", "y"), split_axis=0, concat_axis=0, tiled=True)


def per_device(
    inputs, gate_grad, up_grad, gate_codes, up_codes, gate_scale, up_scale,
    gate_down, gate_lift, up_down, up_lift,
):
    hid = lax.axis_index("hid")
    x, zh, y, core = (lax.axis_index(name) for name in FFN)
    place = jnp.stack([zh, core, hid, x, y])

    both, back_other, back_own = prep(
        place, gate_grad.T, up_grad.T, gate_scale, up_scale, gate_lift, up_lift
    )
    two, one = swap(both, "hid", 2), swap(both, "hid", 1)
    gathered, down = spread(
        inputs, back_own, swap(back_other, "core", 1), gate_down.T, up_down.T
    )

    landed = plane(gathered)
    both, two, one, landed, marked = lax.optimization_barrier(
        (both, two, one, landed, mark(one, two))
    )
    middle = lax.ppermute(both, "hid", [(1, 2), (2, 1)])
    ends = lax.ppermute(two, "hid", [(1, 0), (2, 3)])

    codes = gate_codes.T, up_codes.T
    small = narrow(marked, landed, down)
    small_theirs = swap(small, "zh", 1)
    other1, own1, grads1 = product((both, one, two), 1, *codes)
    middle, ends, small_theirs, marked = lax.optimization_barrier(
        (middle, ends, small_theirs, mark(middle, ends, small_theirs))
    )
    other2, own2, grads2 = product((middle, ends), 2, *codes)
    own2, small_theirs = lax.optimization_barrier((own2, small_theirs))
    sums = add_pairs(
        marked, place, own1, swap(other1, "core", 1), own2, swap(other2, "core", 1)
    )

    parts = gather_over(join_halves(small, small_theirs), "hid")
    marked, parts = lax.optimization_barrier((sums, parts))
    kept = plane(sums.reshape(256, FEATS)).astype(F32).reshape(16, 16, FEATS).sum(0)
    low, adapter, keep, give = joined(marked, place, parts, landed, down)
    low_other = swap(low, "core", 1)
    half = (keep + swap(give, "core", 1)).astype(BF16)
    mine = half.astype(F32) + swap(half, "zh", 1).astype(F32)
    theirs = swap(mine, "core", 1)
    gate_reducer, up_reducer = (jnp.where(core == k, mine, theirs) for k in range(2))
    gate_expander, up_expander = expander(
        place, low_other, low, grads1, grads2, gate_scale, up_scale
    )
    arrived = swap(kept[:8].astype(BF16), "zh", 1)
    rows = (kept[8:] + arrived.astype(F32) + adapter).astype(BF16)
    return rows, gate_reducer.T, gate_expander, up_reducer.T, up_expander


def solution(mesh):
    whole = Mesh(mesh.devices.reshape(4, 4, 2, 4, 2), ("hid",) + FFN)
    placed = (
        P(FFN, "hid"), P("hid", FFN), P("hid", FFN), P("hid", FFN), P("hid", FFN),
        P(FFN), P(FFN), P("hid", None), P(None, FFN), P("hid", None), P(None, FFN),
    )
    return jax.shard_map(
        per_device,
        mesh=whole,
        in_specs=placed,
        out_specs=(P(FFN, "hid"), P("hid", None), P(None, FFN), P("hid", None), P(None, FFN)),
        check_vma=False,
    )
```
